512 devices in a mesh: ctx: 64 (over z, x), head: 8 (over y, core).
Axes of the slice: x: 4, y: 4, z: 16, core: 2. Of those that a mesh axis runs over, the one named last changes fastest.
Arguments:
- inputs: bfloat16 [32768, 4096], P('ctx', 'head'), may hold values from -6 to 6
- w_in: bfloat16 [4096, 4096], P('ctx', 'head'), may hold values from -0.09375 to 0.09375
- b_rows: bfloat16 [32768, 128], P('ctx'), may hold values from -0.5 to 0.5
- c_rows: bfloat16 [32768, 128], P('ctx'), may hold values from -0.5 to 0.5
- log_decay: float32 [64, 32768], P('head', 'ctx'), may hold values from -2.09375 to 0, as said below
- skip_gain: float32 [64], P('head'), may hold values from 0.5 to 2
- grad_out: bfloat16 [32768, 4096], P('ctx', 'head'), may hold values from -6 to 6
Outputs:
- grad_inputs: bfloat16 [32768, 4096], P('ctx', 'head')
- grad_b: float32 [32768, 128], P('ctx')
- grad_c: float32 [32768, 128], P('ctx')
- grad_log_decay: float32 [64, 32768], P('head', 'ctx')
The draws below stay inside these ranges and needn't reach their ends.
Inputs may be any that keep to these rules, and one draw needn't show every extreme that they name: log_decay is negative.
All inputs are finite; a program needn't handle non-finite values.
Results may differ from the reference program's by a relative error of at most 0.017.
Values may be sent and summed in bfloat16 or wider, within the bound.
A program may use at most 128 MiB of HBM per device.

```python
import math
import jax
import jax.numpy as jnp
from jax import lax

D = 4096
SSD_HEAD_COUNT = 64
P_SIZE = 64
N = 128
SPAN = 256
TOKEN_COUNT = 32768
N_HEAD = 8


def draw_log_decay(key, part):
    key = jax.random.fold_in(key, 17)
    random_subkeys = jax.random.split(key, 8)
    slow_cut = 0.4
    middle_cut = 0.75
    blocks = TOKEN_COUNT // SPAN
    class_draw = jax.random.uniform(random_subkeys[0], (SSD_HEAD_COUNT, 1))
    is_slow = class_draw < slow_cut
    is_middle = jnp.logical_and(class_draw >= slow_cut, class_draw < middle_cut)
    slow_rate = jnp.exp(jax.random.uniform(random_subkeys[1], (SSD_HEAD_COUNT, 1), minval=jnp.log(0.1), maxval=jnp.log(0.4))) / TOKEN_COUNT
    fast_rate = 1.0 / (SPAN * jnp.exp(jax.random.uniform(random_subkeys[2], (SSD_HEAD_COUNT, 1), minval=jnp.log(0.125), maxval=jnp.log(0.2))))
    middle_rate = 1.0 / (SPAN * jnp.exp(jax.random.uniform(random_subkeys[7], (SSD_HEAD_COUNT, 1), minval=jnp.log(0.4), maxval=jnp.log(0.65))))
    base_rate = jnp.where(is_slow, slow_rate, jnp.where(is_middle, middle_rate, fast_rate))
    factor_low = jnp.where(is_middle, jnp.log(0.75), jnp.log(0.5))
    factor_high = jnp.where(is_middle, jnp.log(1.5), jnp.log(2.0))
    factor_draw = jax.random.uniform(random_subkeys[3], (SSD_HEAD_COUNT, blocks, 1))
    block_factor = jnp.exp(factor_low[:, :, None] + factor_draw * (factor_high - factor_low)[:, :, None])
    token_factor = jax.random.uniform(random_subkeys[4], (SSD_HEAD_COUNT, blocks, SPAN), minval=0.5, maxval=1.5)
    decay_speeds = (base_rate[:, :, None] * block_factor * token_factor).reshape(SSD_HEAD_COUNT, TOKEN_COUNT)
    surge_location = jax.random.randint(random_subkeys[5], (SSD_HEAD_COUNT, 2, 1), 0, TOKEN_COUNT)
    token_offsets = lax.broadcasted_iota(jnp.int32, (SSD_HEAD_COUNT, 2, TOKEN_COUNT), 2)
    surge_length = jnp.log(jax.random.uniform(random_subkeys[6], (SSD_HEAD_COUNT, 2, 1), minval=0.5, maxval=0.8))
    surge_events = jnp.sum(jnp.where(token_offsets == surge_location, surge_length, 0.0), axis=1)
    return (surge_events - decay_speeds).astype(jnp.float32)


def steps_of(own_key, shape, cuts, low, high):
    level, own = 1.0, jax.random.fold_in(own_key, 6)
    for axis_at, shards_of in cuts:
        steps = jnp.exp(jax.random.uniform(jax.random.fold_in(own, axis_at), (shards_of,), jnp.float32, low / len(cuts), high / len(cuts)))
        level = level * jnp.repeat(steps, shape[axis_at] // shards_of).reshape([-1 if axis == axis_at else 1 for axis in range(len(shape))])
    return level


def centred(own_key, dims, scale, bound, cuts=(), dtype=jnp.bfloat16):
    result = scale * jax.random.normal(own_key, dims, jnp.float32)
    if cuts:
        result = result * steps_of(own_key, dims, cuts, -0.22, 0.18)
    return jnp.clip(result, -bound, bound).astype(dtype)


def setup_inputs(seed: int = 0) -> dict:
    arg_keys = jax.random.split(jax.random.key(seed), 8)
    inputs = centred(arg_keys[0], (TOKEN_COUNT, D), 1.0, 6.0, ((0, 64), (1, 8)))
    w_in = centred(arg_keys[1], (D, SSD_HEAD_COUNT * P_SIZE), D ** -0.5, 0.09375, ((0, 64), (1, 8)))
    b_rows = centred(arg_keys[2], (TOKEN_COUNT, N), 0.08, 0.5, ((0, 64),))
    c_rows = centred(arg_keys[3], (TOKEN_COUNT, N), 0.08, 0.5, ((0, 64),))
    log_decay = draw_log_decay(jax.random.fold_in(arg_keys[7], 71), 0)
    skip_gain = jnp.clip(jnp.exp(math.log(2.0) - 1.3862944 * jax.random.uniform(arg_keys[5], (SSD_HEAD_COUNT,), jnp.float32) ** steps_of(arg_keys[5], (SSD_HEAD_COUNT,), ((0, 8),), -0.2, 0.2)), 0.5, 2.0)
    grad_out = centred(arg_keys[6], (TOKEN_COUNT, SSD_HEAD_COUNT * P_SIZE), 1.0, 6.0, ((0, 64), (1, 8)))
    return dict(inputs=inputs, w_in=w_in, b_rows=b_rows, c_rows=c_rows, log_decay=log_decay, skip_gain=skip_gain, grad_out=grad_out)


exact_precision = lax.Precision.HIGHEST

def span_state(x_rows, b_rows, log_decay):
    length = x_rows.shape[0]
    heads = log_decay.shape[0]
    x_heads = x_rows.reshape(length, heads, -1)
    running = jnp.cumsum(log_decay, axis=1)
    to_end = jnp.exp(running[:, -1:] - running)
    own_state = jnp.einsum('shp,sn->hpn', x_heads * to_end.T[:, :, None], b_rows, precision=exact_precision)
    return (jnp.exp(running[:, -1]), own_state)

def span_forward(x_rows, b_rows, c_rows, log_decay, state_in, skip_gain):
    length = x_rows.shape[0]
    heads = log_decay.shape[0]
    x_heads = x_rows.reshape(length, heads, -1)
    running = jnp.cumsum(log_decay, axis=1)
    later = lax.broadcasted_iota(jnp.int32, (length, length), 0)
    earlier = lax.broadcasted_iota(jnp.int32, (length, length), 1)
    causal = (later >= earlier)[None]
    spread = running[:, :, None] - running[:, None, :]
    kernel = jnp.where(causal, jnp.exp(jnp.where(causal, spread, 0.0)), 0.0)
    scores = jnp.dot(c_rows, b_rows.T, precision=exact_precision)
    inner = jnp.einsum('hts,shp->thp', kernel * scores[None], x_heads, precision=exact_precision)
    from_state = jnp.einsum('tn,hpn->thp', c_rows, state_in, precision=exact_precision)
    from_state = from_state * jnp.exp(running).T[:, :, None]
    outputs = inner + from_state + skip_gain[None, :, None] * x_heads
    retained, own_state = span_state(x_rows, b_rows, log_decay)
    state_out = retained[:, None, None] * state_in + own_state
    return (outputs.reshape(length, -1), state_out)

def boundary_grad(c_rows, log_decay, g_rows):
    length = g_rows.shape[0]
    heads = log_decay.shape[0]
    g_heads = g_rows.reshape(length, heads, -1)
    running = jnp.cumsum(log_decay, axis=1)
    return jnp.einsum('thp,tn->hpn', g_heads * jnp.exp(running).T[:, :, None], c_rows, precision=exact_precision)

def reference(inputs, w_in, b_rows, c_rows, log_decay, skip_gain, grad_out):
    x_rows = jnp.dot(inputs, w_in, preferred_element_type=jnp.float32).astype(jnp.bfloat16)
    x_float = lax.optimization_barrier(x_rows).astype(jnp.float32)
    blocks = TOKEN_COUNT // SPAN
    x_blocks = x_float.reshape(blocks, SPAN, SSD_HEAD_COUNT * P_SIZE)
    b_blocks = b_rows.astype(jnp.float32).reshape(blocks, SPAN, N)
    c_blocks = c_rows.astype(jnp.float32).reshape(blocks, SPAN, N)
    g_blocks = grad_out.astype(jnp.float32).reshape(blocks, SPAN, SSD_HEAD_COUNT * P_SIZE)
    d_blocks = log_decay.reshape(SSD_HEAD_COUNT, blocks, SPAN).transpose(1, 0, 2)

    def state_of(element):
        return span_state(element[0], element[1], element[2])
    retained, own_states = lax.map(state_of, (x_blocks, b_blocks, d_blocks))
    empty = jnp.zeros((SSD_HEAD_COUNT, P_SIZE, N), jnp.float32)

    def advance(state, element):
        return (element[0][:, None, None] * state + element[1], state)
    _, states_in = lax.scan(advance, empty, (retained, own_states))

    def grad_of(element):
        return boundary_grad(element[0], element[1], element[2])
    state_grads = lax.map(grad_of, (c_blocks, d_blocks, g_blocks))

    def retreat(state, element):
        return (element[1] + element[0][:, None, None] * state, state)
    _, states_out_grad = lax.scan(retreat, empty, (retained, state_grads), reverse=True)

    def block_grads(element):
        x_block, b_block, c_block, d_block, state_in, g_block, state_grad_out = element

        def local_forward(x_value, b_value, c_value, d_value):
            return span_forward(x_value, b_value, c_value, d_value, state_in, skip_gain)
        _, pullback = jax.vjp(local_forward, x_block, b_block, c_block, d_block)
        return pullback((g_block, state_grad_out))
    grad_x, grad_b, grad_c, grad_d = lax.map(block_grads, (x_blocks, b_blocks, c_blocks, d_blocks, states_in, g_blocks, states_out_grad))
    grad_x_rows = grad_x.reshape(TOKEN_COUNT, SSD_HEAD_COUNT * P_SIZE).astype(jnp.bfloat16)
    columns = SSD_HEAD_COUNT * P_SIZE // N_HEAD
    summed = jnp.zeros((TOKEN_COUNT, D), jnp.float32)
    for head_group in range(N_HEAD):
        grad_part = grad_x_rows[:, head_group * columns:(head_group + 1) * columns]
        weight_part = w_in[:, head_group * columns:(head_group + 1) * columns]
        product = lax.dot_general(grad_part, weight_part, (((1,), (1,)), ((), ())), preferred_element_type=jnp.float32)
        summed = summed + product.astype(jnp.bfloat16).astype(jnp.float32)
    grad_inputs = summed.astype(jnp.bfloat16)
    grad_log_decay = grad_d.transpose(1, 0, 2).reshape(SSD_HEAD_COUNT, TOKEN_COUNT)
    return (grad_inputs, grad_b.reshape(TOKEN_COUNT, N), grad_c.reshape(TOKEN_COUNT, N), grad_log_decay)
```

```python
import jax
import jax.numpy as jnp
from jax import lax
from jax.experimental import pallas as pl
from jax.experimental.pallas import tpu as pltpu
from jax.sharding import PartitionSpec as P

MESH = pl.DeviceIdType.MESH
BF = jnp.bfloat16
F32 = jnp.float32
EXACT = lax.Precision.HIGHEST
NX, NY, NZ = 4, 4, 16
SPAN = 256
T = 512
CA = 256
CB = 512 - CA
NEG = -1e30


def mm(a, b, precision=None):
    return lax.dot_general(a, b, (((1,), (0,)), ((), ())), precision=precision, preferred_element_type=F32)


def mm_nt(a, b, precision=None):
    return lax.dot_general(a, b, (((1,), (1,)), ((), ())), precision=precision, preferred_element_type=F32)


def mm_tn(a, b):
    return lax.dot_general(a, b, (((0,), (0,)), ((), ())), preferred_element_type=F32)


def iota(shape, dim):
    return lax.broadcasted_iota(jnp.int32, shape, dim)


N_SEND = 240
N_RECV = 264


def kernel(
    inp_ref, w_ref, b_ref, c_ref, ld_ref, sk_ref, g_ref,
    gi_ref, gb_ref, gc_ref, gld_ref,
    wbuf, inpb, pbuf, sibr, yfar, ynear, lt_ref, mt_ref, gxf, gx, te_ref, v_ref, xacc, x_ref, ex_ref,
    rr_ref, rc_ref, a_ref, adev, ax_ref, az_ref,
    gst, est, qs, ss, sx_ref, xr, tz, zr, zo, zp, bo_ref, br_ref,
    dmt, drow, dcol, pr, prr, pfin, pfull,
    send_sem, recv_sem,
):
    ctx = lax.axis_index("ctx")
    head = lax.axis_index("head")
    z, x = ctx // NX, ctx % NX
    y, c = head // 2, head % 2

    def at_x(d):
        return (z * NX + (x + d) % NX, head)

    def at_z(d):
        return (((z + d) % NZ) * NX + x, head)

    def at_y(d):
        return (ctx, ((y + d) % NY) * 2 + c)

    sib = (ctx, y * 2 + (1 - c))

    def at_head(d):
        return (ctx, (head + d) % 8)

    counts = {"s": 0, "r": 0}
    sent = []

    def recv_slots(n):
        base = counts["r"]
        counts["r"] += n
        return base

    def copy(src, dst, slot, device):
        k = counts["s"]
        counts["s"] += 1
        d = pltpu.make_async_remote_copy(
            src_ref=src, dst_ref=dst, send_sem=send_sem.at[k], recv_sem=recv_sem.at[slot],
            device_id=device, device_id_type=MESH,
        )
        d.start()
        sent.append(d)

    def arrived(dst, slot):
        pltpu.make_async_remote_copy(
            src_ref=dst, dst_ref=dst, send_sem=send_sem.at[0], recv_sem=recv_sem.at[slot],
            device_id=sib, device_id_type=MESH,
        ).wait_recv()

    barrier = pltpu.get_barrier_semaphore()
    peers = [at_x(d) for d in range(1, NX)] + [at_z(d) for d in range(1, NZ)] + [at_head(d) for d in range(1, 8)]
    for peer in peers:
        pl.semaphore_signal(barrier, inc=1, device_id=peer, device_id_type=MESH)
    pl.semaphore_wait(barrier, len(peers))

    def wrows(zz, xx):
        return pl.ds(pl.multiple_of((zz * NX + xx) * 64, 64), 64)

    def wgroup(zz):
        return pl.ds(pl.multiple_of(zz * 256, 256), 256)

    colsA, colsB = pl.ds(0, CA), pl.ds(CA, CB)
    HB = 128 * ((CB // 2 + 127) // 128)
    colsB1, colsB2 = pl.ds(CA, HB), pl.ds(CA + HB, CB - HB)
    w0 = recv_slots(4)
    for d in (1, 3, 2):
        copy(w_ref, wbuf.at[wrows(z, x), :], w0 + d, at_x(d))
    bR, bL, aR, aL = recv_slots(9), recv_slots(9), recv_slots(9), recv_slots(9)
    copy(w_ref.at[:, colsB], wbuf.at[wrows(z, x), colsB], bR + 1, at_z(1))
    copy(w_ref.at[:, colsB], wbuf.at[wrows(z, x), colsB], bL + 1, at_z(NZ - 1))

    half = (pl.ds(0, 256), pl.ds(256, 256))
    iR, iL, iF, iS = recv_slots(2), recv_slots(2), recv_slots(2), recv_slots(8)

    def ihead(d):
        return ((y + d) % NY) * 2 + c

    copy(inp_ref.at[:, half[0]], inpb.at[head, :, half[0]], iR + 0, at_y(1))
    copy(inp_ref.at[:, half[1]], inpb.at[head, :, half[1]], iL + 1, at_y(3))
    copy(inp_ref.at[:, half[1]], inpb.at[head, :, half[1]], iR + 1, at_y(1))
    copy(inp_ref.at[:, half[0]], inpb.at[head, :, half[0]], iL + 0, at_y(3))
    copy(inp_ref, inpb.at[head], iS + 0, sib)

    wbuf[wrows(z, x), :] = w_ref[...]
    inpb[head] = inp_ref[...]

    def input_pass(part):
        left, right, far = ihead(3), ihead(1), ihead(2)
        if part == 0:
            arrived(inpb.at[left, :, half[0]], iR + 0)
            copy(inpb.at[left, :, half[0]], inpb.at[left, :, half[0]], iF + 0, at_y(1))
            arrived(inpb.at[right, :, half[1]], iL + 1)
            copy(inpb.at[right, :, half[1]], inpb.at[right, :, half[1]], iF + 1, at_y(3))
            copy(inpb.at[left, :, half[0]], inpb.at[left, :, half[0]], iS + 1, sib)
            copy(inpb.at[right, :, half[1]], inpb.at[right, :, half[1]], iS + 2, sib)
        if part == 1:
            arrived(inpb.at[left, :, half[1]], iR + 1)
            copy(inpb.at[left, :, half[1]], inpb.at[left, :, half[1]], iS + 3, sib)
            arrived(inpb.at[right, :, half[0]], iL + 0)
            copy(inpb.at[right, :, half[0]], inpb.at[right, :, half[0]], iS + 4, sib)
        if part == 2:
            for k in (0, 1):
                arrived(inpb.at[far, :, half[k]], iF + k)
                copy(inpb.at[far, :, half[k]], inpb.at[far, :, half[k]], iS + 5 + k, sib)
        if part == 3:
            def other(d):
                return ((y + d) % NY) * 2 + (1 - c)
            arrived(inpb.at[other(0)], iS + 0)
            arrived(inpb.at[other(3), :, half[0]], iS + 1)
            arrived(inpb.at[other(1), :, half[1]], iS + 2)
            arrived(inpb.at[other(3), :, half[1]], iS + 3)
            arrived(inpb.at[other(1), :, half[0]], iS + 4)
            for k in (0, 1):
                arrived(inpb.at[other(2), :, half[k]], iS + 5 + k)

    def w_start():
        for d in (1, 2, 3):
            arrived(wbuf.at[wrows(z, (x + NX - d) % NX), :], w0 + d)
        copy(wbuf.at[wgroup(z), colsA], wbuf.at[wgroup(z), colsA], aR + 1, at_z(1))
        copy(wbuf.at[wgroup(z), colsA], wbuf.at[wgroup(z), colsA], aL + 1, at_z(NZ - 1))

    xslots = {}

    def w_across(key, zz):
        base = recv_slots(4)
        xslots[key] = base
        blk = wbuf.at[wrows(zz, x), colsB]
        copy(blk, blk, base + 0, at_x(1))
        copy(blk, blk, base + 1, at_x(3))

    def w_across2(key, zz):
        base = xslots[key]
        left, right = (x + 3) % NX, (x + 1) % NX
        arrived(wbuf.at[wrows(zz, left), colsB], base + 0)
        blk = wbuf.at[wrows(zz, left), colsB1]
        copy(blk, blk, base + 2, at_x(1))
        arrived(wbuf.at[wrows(zz, right), colsB], base + 1)
        blk = wbuf.at[wrows(zz, right), colsB2]
        copy(blk, blk, base + 3, at_x(3))

    def w_step(s):
        zr_, zl_ = (z + NZ - s) % NZ, (z + s) % NZ
        if s <= 8:
            blk = wbuf.at[wgroup(zr_), colsA]
            arrived(blk, aR + s)
            if s < 8:
                copy(blk, blk, aR + s + 1, at_z(1))
        if s <= 7:
            blk = wbuf.at[wgroup(zl_), colsA]
            arrived(blk, aL + s)
            if s < 7:
                copy(blk, blk, aL + s + 1, at_z(NZ - 1))
        if s <= 7:
            blk = wbuf.at[wrows(zr_, x), colsB]
            arrived(blk, bR + s)
            if s < 7:
                copy(blk, blk, bR + s + 1, at_z(1))
            w_across(("R", s), zr_)
        if s <= 8:
            blk = wbuf.at[wrows(zl_, x), colsB]
            arrived(blk, bL + s)
            if s < 8:
                copy(blk, blk, bL + s + 1, at_z(NZ - 1))
            w_across(("L", s), zl_)
        if s >= 2:
            w_late(s - 1)

    def w_late(s):
        if s <= 7:
            w_across2(("R", s), (z + NZ - s) % NZ)
        if s <= 8:
            w_across2(("L", s), (z + s) % NZ)

    def w_end():
        w_late(8)
        far = (x + 2) % NX
        for (side, s), base in xslots.items():
            zz = (z + NZ - s) % NZ if side == "R" else (z + s) % NZ
            arrived(wbuf.at[wrows(zz, far), colsB1], base + 2)
            arrived(wbuf.at[wrows(zz, far), colsB2], base + 3)

    lane = iota((SPAN, 128), 1)
    low = lane < 64
    lowrow = iota((1, 128), 1) < 64
    ti, tj = iota((SPAN, SPAN), 0), iota((SPAN, SPAN), 1)
    upto = ti <= tj

    def pair(col, i):
        return jnp.where(low, col[:, 2 * i:2 * i + 1], col[:, 2 * i + 1:2 * i + 2])

    def pair_row(row, i):
        return jnp.where(lowrow, row[:, 2 * i:2 * i + 1], row[:, 2 * i + 1:2 * i + 2])

    def first(sp):
        rows = pl.ds(sp * SPAN, SPAN)
        rr = mm(ld_ref[:, rows], upto.astype(F32), EXACT)
        rc = jnp.concatenate([rr, jnp.zeros((120, SPAN), F32)], 0).T
        rr_ref[sp] = rr
        rc_ref[sp] = rc
        last = rc[SPAN - 1:SPAN, :]
        ec, tc, al = jnp.exp(rc), jnp.exp(last - rc), jnp.exp(last)
        ct = c_ref[rows, :].T
        for i in range(4):
            cols = pl.ds(i * 128, 128)
            v = (g_ref[rows, cols].astype(F32) * pair(ec, i)).astype(BF)
            v_ref[rows, cols] = v
            te_ref[rows, cols] = pair(tc, i)
            a_ref[sp, i] = jnp.broadcast_to(pair_row(al, i), (8, 128))
            gst[sp, i] = mm(ct, v)
        mt_ref[sp] = mm_nt(b_ref[rows, :], c_ref[rows, :])

    def unit1(sp, i):
        rows, cols = pl.ds(sp * SPAN, SPAN), pl.ds(i * 128, 128)
        g2 = g_ref[rows, cols]
        mt = mt_ref[sp]
        parts = []
        for k in (0, 1):
            h = 2 * i + k
            diff = rr_ref[sp, h:h + 1, :] - rc_ref[sp, :, h:h + 1]
            lt = jnp.exp(jnp.where(upto, diff, NEG))
            lt_ref[sp * 8 + h] = lt
            parts.append(mm((lt * mt).astype(BF), g2))
        skip = jnp.where(lowrow, sk_ref[2 * i], sk_ref[2 * i + 1])
        gxf[rows, cols] = jnp.where(low, parts[0], parts[1]) + skip * g2.astype(F32)

    def scan_x_send(which, state):
        base = recv_slots(4)
        for i in range(4):
            sx_ref[which, i] = state(i).astype(BF)
        for d in (1, 3, 2):
            to = (x + d) % NX
            copy(sx_ref.at[which, to], xr.at[which, x], base + d, at_x(d))
        xr[which, x] = sx_ref[which, x]
        return base

    def scan_x_wait(which, base):
        for d in (1, 2, 3):
            arrived(xr.at[which, (x + NX - d) % NX], base + d)

    def scan_z_send(which):
        base = recv_slots(16)
        for d in range(1, NZ):
            to = (z + d) % NZ
            copy(tz.at[which, to], zr.at[which, z], base + d, at_z(d))
        zr[which, z] = tz[which, z]
        return base

    def scan_z_wait(which, base):
        for d in range(1, NZ):
            arrived(zr.at[which, (z + NZ - d) % NZ], base + d)

    def scan_z_back(which):
        base = recv_slots(16)
        for d in range(1, NZ):
            to = (z + d) % NZ
            copy(zo.at[which, to], zp.at[which, z], base + d, at_z(d))
        zp[which, z] = zo[which, z]
        return base

    def scan_z_back_wait(which, base):
        for d in range(1, NZ):
            arrived(zp.at[which, (z + NZ - d) % NZ], base + d)

    def scan_x_back(which):
        base = recv_slots(4)
        for d in (1, 3, 2):
            to = (x + d) % NX
            copy(bo_ref.at[which, to], br_ref.at[which, x], base + d, at_x(d))
        br_ref[which, x] = bo_ref[which, x]
        return base

    def scan_x_back_wait(which, base):
        for d in (1, 2, 3):
            arrived(br_ref.at[which, (x + NX - d) % NX], base + d)

    marks = {}

    def ret_x():
        base = recv_slots(4)
        for i in range(4):
            adev[i] = a_ref[0, i] * a_ref[1, i]
        for d in (1, 3, 2):
            to = (x + d) % NX
            copy(adev.at[to], ax_ref.at[x], base + d, at_x(d))
        ax_ref[x] = adev[x]
        marks["ax"] = base

    def ret_z():
        for d in (1, 2, 3):
            arrived(ax_ref.at[(x + NX - d) % NX], marks["ax"] + d)
        base = recv_slots(16)
        adev[4] = ax_ref[0] * ax_ref[1] * ax_ref[2] * ax_ref[3]
        for d in range(1, NZ):
            copy(adev.at[4], az_ref.at[z], base + d, at_z(d))
        az_ref[z] = adev[4]
        marks["az"] = base

    def ret_wait():
        for d in range(1, NZ):
            arrived(az_ref.at[(z + NZ - d) % NZ], marks["az"] + d)

    def ret(k):
        return ax_ref[k][0:1, :]

    def put_total(which, total):
        for k in range(NZ):
            tz[which, k] = total[8 * k:8 * k + 8, :]

    def bscan(part):
        if part == 0:
            marks["b0"] = scan_x_send(0, lambda i: gst[0, i] + a_ref[0, i][0:1, :] * gst[1, i])
        if part == 1:
            scan_x_wait(0, marks["b0"])
            total = xr[0, 3].astype(F32)
            for k in (2, 1, 0):
                total = xr[0, k].astype(F32) + ret(k) * total
            put_total(0, total)
            marks["b1"] = scan_z_send(0)
        if part == 2:
            ret_wait()
            scan_z_wait(0, marks["b1"])
            q = jnp.zeros((8, 128), F32)
            for k in range(NZ - 1, -1, -1):
                zo[0, k] = q
                q = zr[0, k] + az_ref[k] * q
            marks["b2"] = scan_z_back(0)
        if part == 3:
            scan_z_back_wait(0, marks["b2"])
            q = jnp.concatenate([zp[0, k] for k in range(NZ)], 0)
            for k in (3, 2, 1, 0):
                bo_ref[0, k] = q.astype(BF)
                if k:
                    q = xr[0, k].astype(F32) + ret(k) * q
            marks["b3"] = scan_x_back(0)
        if part == 4:
            scan_x_back_wait(0, marks["b3"])
            for i in range(4):
                cols = pl.ds(i * 128, 128)
                q = br_ref[0, i]
                qs[1, :, cols] = q
                qs[0, :, cols] = (gst[1, i] + a_ref[1, i][0:1, :] * q.astype(F32)).astype(BF)

    def fscan(part):
        if part == 0:
            marks["f0"] = scan_x_send(1, lambda i: a_ref[1, i][0:1, :] * est[0, i] + est[1, i])
        if part == 1:
            scan_x_wait(1, marks["f0"])
            total = xr[1, 0].astype(F32)
            for k in (1, 2, 3):
                total = xr[1, k].astype(F32) + ret(k) * total
            put_total(1, total)
            marks["f1"] = scan_z_send(1)
        if part == 2:
            scan_z_wait(1, marks["f1"])
            s = jnp.zeros((8, 128), F32)
            for k in range(NZ):
                zo[1, k] = s
                s = zr[1, k] + az_ref[k] * s
            marks["f2"] = scan_z_back(1)
        if part == 3:
            scan_z_back_wait(1, marks["f2"])
            s = jnp.concatenate([zp[1, k] for k in range(NZ)], 0)
            for k in range(NX):
                bo_ref[1, k] = s.astype(BF)
                if k < NX - 1:
                    s = xr[1, k].astype(F32) + ret(k) * s
            marks["f3"] = scan_x_back(1)
        if part == 4:
            scan_x_back_wait(1, marks["f3"])
            for i in range(4):
                cols = pl.ds(i * 128, 128)
                s = br_ref[1, i]
                ss[0, :, cols] = s
                ss[1, :, cols] = (a_ref[0, i][0:1, :] * s.astype(F32) + est[0, i]).astype(BF)

    def finish_gx(sp):
        rows = pl.ds(sp * SPAN, SPAN)
        gx[rows, :] = (gxf[rows, :] + te_ref[rows, :] * mm(b_ref[rows, :], qs[sp])).astype(BF)

    def project():
        xacc[...] = jnp.zeros_like(xacc)

        def one(j, carry):
            xacc[...] += mm(inpb[j], wbuf[pl.ds(pl.multiple_of(j * 512, 512), 512), :])
            return carry

        lax.fori_loop(0, 8, one, 0)
        xb = xacc[...].astype(BF)
        x_ref[...] = xb
        ex_ref[...] = (te_ref[...] * xb.astype(F32)).astype(BF)
        for sp in range(2):
            rows = pl.ds(sp * SPAN, SPAN)
            bt = b_ref[rows, :].T
            for i in range(4):
                est[sp, i] = mm(bt, ex_ref[rows, pl.ds(i * 128, 128)])

    rS = recv_slots(4)

    def wblock(j):
        return wbuf[pl.ds(pl.multiple_of(j * 512, 512), 512), :]

    def rs_sib():
        for d in (2, 1, 3, 0):
            j = ((y + d) % NY) * 2 + (1 - c)
            pbuf[j] = mm_nt(gx[...], wblock(j)).astype(BF)
            copy(pbuf.at[j], sibr.at[(y + d) % NY], rS + d, sib)

    rF, rN = recv_slots(2), recv_slots(4)

    def rs_own(d):
        yy = (y + d) % NY
        j = yy * 2 + c
        own = mm_nt(gx[...], wblock(j))
        arrived(sibr.at[yy], rS + d)
        pbuf[j] = (own + sibr[yy].astype(F32)).astype(BF)
        if d == 2:
            copy(pbuf.at[j, :, half[1]], yfar.at[:, half[1]], rF + 1, at_y(1))
            copy(pbuf.at[j, :, half[0]], yfar.at[:, half[0]], rF + 0, at_y(3))
        if d == 1:
            copy(pbuf.at[j, :, half[0]], ynear.at[0, :, half[0]], rN + 0, at_y(1))
        if d == 3:
            copy(pbuf.at[j, :, half[1]], ynear.at[1, :, half[1]], rN + 1, at_y(3))

    def rs_pass():
        j = ((y + 1) % NY) * 2 + c
        arrived(yfar.at[:, half[1]], rF + 1)
        pbuf[j, :, 256:512] = (pbuf[j, :, 256:512].astype(F32) + yfar[:, 256:512].astype(F32)).astype(BF)
        copy(pbuf.at[j, :, half[1]], ynear.at[0, :, half[1]], rN + 2, at_y(1))
        j = ((y + 3) % NY) * 2 + c
        arrived(yfar.at[:, half[0]], rF + 0)
        pbuf[j, :, 0:256] = (pbuf[j, :, 0:256].astype(F32) + yfar[:, 0:256].astype(F32)).astype(BF)
        copy(pbuf.at[j, :, half[0]], ynear.at[1, :, half[0]], rN + 3, at_y(3))

    def rs_end():
        arrived(ynear.at[0, :, half[0]], rN + 0)
        arrived(ynear.at[1, :, half[1]], rN + 1)
        arrived(ynear.at[0, :, half[1]], rN + 2)
        arrived(ynear.at[1, :, half[0]], rN + 3)
        gi_ref[...] = (
            pbuf[head].astype(F32) + ynear[0].astype(F32) + ynear[1].astype(F32)
        ).astype(BF)

    def unit2(sp):
        rows = pl.ds(sp * SPAN, SPAN)
        dmt[sp] = jnp.zeros((SPAN, SPAN), F32)
        dcol[sp] = jnp.zeros((SPAN, 128), F32)

        def one(i, carry):
            cols = pl.ds(pl.multiple_of(i * 128, 128), 128)
            g2, x2 = g_ref[rows, cols], x_ref[rows, cols]
            mt = mt_ref[sp]
            for k in (0, 1):
                h = 2 * i + k
                xm = jnp.where(low if k == 0 else jnp.logical_not(low), x2, jnp.zeros_like(x2))
                p = mm_nt(xm, g2) * lt_ref[sp * 8 + h]
                dmt[sp] += p
                wm = p * mt
                drow[sp, pl.ds(h, 1), :] = jnp.sum(wm, axis=0, keepdims=True)
                dcol[sp] += jnp.where(lane == h, jnp.sum(wm, axis=1, keepdims=True), 0.0)
            return carry

        lax.fori_loop(0, 4, one, 0)

    ind = (iota((8, 512), 1) // 64 == iota((8, 512), 0)).astype(BF)

    def head_sums(value):
        hi = value.astype(BF)
        lo = (value - hi.astype(F32)).astype(BF)
        return mm_nt(ind, hi) + mm_nt(ind, lo)

    def grad_b_part(sp):
        rows = pl.ds(sp * SPAN, SPAN)
        pr[0, rows, :] = (mm(dmt[sp].astype(BF), c_ref[rows, :]) + mm_nt(ex_ref[rows, :], qs[sp])).astype(BF)

    def grad_c_part(sp):
        rows = pl.ds(sp * SPAN, SPAN)
        pr[1, rows, :] = (
            mm_tn(dmt[sp].astype(BF), b_ref[rows, :]) + mm_nt(v_ref[rows, :], ss[sp])
        ).astype(BF)

    def decay_part(sp):
        rows = pl.ds(sp * SPAN, SPAN)
        u = mm(c_ref[rows, :], ss[sp])
        arow = jnp.concatenate([a_ref[sp, i][0:1, :] for i in range(4)], 1)
        cross = jnp.sum(qs[sp].astype(F32) * ss[sp].astype(F32), axis=0, keepdims=True) * arow
        is_last = iota((SPAN, 512), 0) == SPAN - 1
        vv = v_ref[rows, :].astype(F32) * u + jnp.where(is_last, cross, 0.0)
        tt = te_ref[rows, :] * x_ref[rows, :].astype(F32) * mm(b_ref[rows, :], qs[sp])
        dr = head_sums(vv) + drow[sp] - dcol[sp].T[0:8, :]
        gld_ref[:, rows] = mm(dr, (ti >= tj).astype(F32), EXACT) + mm(head_sums(tt), (ti < tj).astype(F32), EXACT)

    def mine(k):
        return pl.ds(pl.multiple_of(k * 64, 64), 64)

    def ps_send(which):
        base = recv_slots(8)
        for d in range(1, 8):
            to = (head + d) % 8
            copy(pr.at[which, mine(to), :], prr.at[which, head], base + d, at_head(d))
        prr[which, head] = pr[which, mine(head), :]
        return base

    def ps_sum(which, base):
        for d in range(1, 8):
            arrived(prr.at[which, (head + 8 - d) % 8], base + d)
        total = prr[which, 0].astype(F32)
        for k in range(1, 8):
            total = total + prr[which, k].astype(F32)
        pfin[which] = total.astype(BF)
        base = recv_slots(8)
        for d in range(1, 8):
            copy(pfin.at[which], pfull.at[which, mine(head), :], base + d, at_head(d))
        pfull[which, mine(head), :] = pfin[which]
        return base

    def ps_end(which, base, out):
        for d in range(1, 8):
            arrived(pfull.at[which, mine((head + 8 - d) % 8), :], base + d)
        out[...] = pfull[which].astype(F32)

    first(0)
    first(1)
    ret_x()
    bscan(0)
    w_start()
    ret_z()
    bscan(1)
    for s in range(1, 9):
        unit1((s - 1) // 4, (s - 1) % 4)
        w_step(s)
        if s == 1:
            bscan(2)
        if s == 2:
            bscan(3)
            input_pass(0)
        if s == 3:
            bscan(4)
            input_pass(1)
        if s == 5:
            input_pass(2)
    input_pass(3)
    finish_gx(0)
    finish_gx(1)
    w_end()
    project()
    fscan(0)
    rs_sib()
    fscan(1)
    rs_own(2)
    fscan(2)
    rs_own(1)
    rs_own(3)
    rs_own(0)
    fscan(3)
    unit2(0)
    rs_pass()
    unit2(1)
    grad_b_part(0)
    grad_b_part(1)
    pb = ps_send(0)
    fscan(4)
    grad_c_part(0)
    grad_c_part(1)
    pc = ps_send(1)
    pb = ps_sum(0, pb)
    decay_part(0)
    pc = ps_sum(1, pc)
    decay_part(1)
    ps_end(0, pb, gb_ref)
    ps_end(1, pc, gc_ref)
    rs_end()
    for d in sent:
        d.wait_send()
    assert counts["s"] <= N_SEND and counts["r"] <= N_RECV, counts


def local(inputs, w_in, b_rows, c_rows, log_decay, skip_gain, grad_out):
    vmem = pl.BlockSpec(memory_space=pltpu.VMEM)
    V = pltpu.VMEM
    return pl.pallas_call(
        kernel,
        out_shape=(
            jax.ShapeDtypeStruct((T, 512), BF),
            jax.ShapeDtypeStruct((T, 128), F32),
            jax.ShapeDtypeStruct((T, 128), F32),
            jax.ShapeDtypeStruct((8, T), F32),
        ),
        in_specs=[vmem] * 5 + [pl.BlockSpec(memory_space=pltpu.SMEM), vmem],
        out_specs=(vmem,) * 4,
        scratch_shapes=[
            V((4096, 512), BF),
            V((8, T, 512), BF),
            V((8, T, 512), BF),
            V((4, T, 512), BF),
            V((T, 512), BF),
            V((2, T, 512), BF),
            V((16, SPAN, SPAN), F32),
            V((2, SPAN, SPAN), F32),
            V((T, 512), F32),
            V((T, 512), BF),
            V((T, 512), F32),
            V((T, 512), BF),
            V((T, 512), F32),
            V((T, 512), BF),
            V((T, 512), BF),
            V((2, 8, SPAN), F32),
            V((2, SPAN, 128), F32),
            V((2, 4, 8, 128), F32),
            V((5, 8, 128), F32),
            V((4, 8, 128), F32),
            V((16, 8, 128), F32),
            V((2, 4, 128, 128), F32),
            V((2, 4, 128, 128), F32),
            V((2, 128, 512), BF),
            V((2, 128, 512), BF),
            V((2, 4, 128, 128), BF),
            V((2, 4, 128, 128), BF),
            V((2, 16, 8, 128), F32),
            V((2, 16, 8, 128), F32),
            V((2, 16, 8, 128), F32),
            V((2, 16, 8, 128), F32),
            V((2, 4, 128, 128), BF),
            V((2, 4, 128, 128), BF),
            V((2, SPAN, SPAN), F32),
            V((2, 8, SPAN), F32),
            V((2, SPAN, 128), F32),
            V((2, T, 128), BF),
            V((2, 8, 64, 128), BF),
            V((2, 64, 128), BF),
            V((2, T, 128), BF),
            pltpu.SemaphoreType.DMA((N_SEND,)),
            pltpu.SemaphoreType.DMA((N_RECV,)),
        ],
        compiler_params=pltpu.CompilerParams(
            collective_id=0, has_side_effects=True, vmem_limit_bytes=52 * 1024 * 1024
        ),
        cost_estimate=pl.CostEstimate(flops=8 * 10**9, bytes_accessed=4 * 10**6, transcendentals=2 * 10**6),
    )(inputs, w_in, b_rows, c_rows, log_decay, skip_gain, grad_out)


def solution(mesh):
    in_specs = (
        P("ctx", "head"),
        P("ctx", "head"),
        P("ctx", None),
        P("ctx", None),
        P("head", "ctx"),
        P("head"),
        P("ctx", "head"),
    )
    out_specs = (P("ctx", "head"), P("ctx", None), P("ctx", None), P("head", "ctx"))
    return jax.shard_map(local, mesh=mesh, in_specs=in_specs, out_specs=out_specs, check_vma=False)
```

```python
import jax
import jax.numpy as jnp
from jax import lax
from jax.experimental import pallas as pl
from jax.experimental.pallas import tpu as pltpu
from jax.sharding import PartitionSpec as P

MESH = pl.DeviceIdType.MESH
BF = jnp.bfloat16
F32 = jnp.float32
EXACT = lax.Precision.HIGHEST
NX, NY, NZ = 4, 4, 16
SPAN = 256
T = 512
NEG = -1e30
Q_FROM = 4
FAR_FIRST = sorted(range(1, NZ), key=lambda d: -min(d, NZ - d))


def mm(a, b, precision=None):
    return lax.dot_general(a, b, (((1,), (0,)), ((), ())), precision=precision, preferred_element_type=F32)


def mm_nt(a, b, precision=None):
    return lax.dot_general(a, b, (((1,), (1,)), ((), ())), precision=precision, preferred_element_type=F32)


def mm_tn(a, b):
    return lax.dot_general(a, b, (((0,), (0,)), ((), ())), preferred_element_type=F32)


def iota(shape, dim):
    return lax.broadcasted_iota(jnp.int32, shape, dim)


N_SEND = 300
N_RECV = 340


def kernel(
    inp_ref, w_ref, b_hbm, c_hbm, ld_hbm, sk_ref, g_hbm,
    gi_hbm, gb_hbm, gc_hbm, gld_hbm,
    b_ref, c_ref, ld_ref, g_ref, gi_ref, gb_ref, gc_ref, gld_ref,
    wbuf, inpb, pbuf, sibr, yfar, ynear, lt_ref, mt_ref, gxf, gx, te_ref, v_ref, xacc, x_ref, ex_ref,
    rr_ref, rc_ref, a_ref, adev, ax_ref, az_ref,
    gst, est, qs, ss, sx_ref, xr, tz, zr, zo, zp, bo_ref, br_ref,
    dmt, drow, dcol, pr, prr, pfin, pfull,
    send_sem, recv_sem, load_sem,
):
    ctx = lax.axis_index("ctx")
    head = lax.axis_index("head")
    z, x = ctx // NX, ctx % NX
    y, c = head // 2, head % 2

    def at_x(d):
        return (z * NX + (x + d) % NX, head)

    def at_z(d):
        return (((z + d) % NZ) * NX + x, head)

    def at_y(d):
        return (ctx, ((y + d) % NY) * 2 + c)

    sib = (ctx, y * 2 + (1 - c))

    def at_head(d):
        return (ctx, (head + d) % 8)

    counts = {"s": 0, "r": 0}
    sent = []

    def recv_slots(n):
        base = counts["r"]
        counts["r"] += n
        return base

    def copy(src, dst, slot, device):
        k = counts["s"]
        counts["s"] += 1
        d = pltpu.make_async_remote_copy(
            src_ref=src, dst_ref=dst, send_sem=send_sem.at[k], recv_sem=recv_sem.at[slot],
            device_id=device, device_id_type=MESH,
        )
        d.start()
        sent.append(d)

    def arrived(dst, slot):
        pltpu.make_async_remote_copy(
            src_ref=dst, dst_ref=dst, send_sem=send_sem.at[0], recv_sem=recv_sem.at[slot],
            device_id=sib, device_id_type=MESH,
        ).wait_recv()

    loads = []
    for src, dst in ((ld_hbm, ld_ref), (c_hbm, c_ref), (g_hbm, g_ref), (b_hbm, b_ref)):
        d = pltpu.make_async_copy(src, dst, load_sem.at[len(loads)])
        d.start()
        loads.append(d)

    barrier = pltpu.get_barrier_semaphore()
    peers = [at_x(d) for d in range(1, NX)] + [at_z(d) for d in range(1, NZ)] + [at_head(d) for d in range(1, 8)]
    for peer in peers:
        pl.semaphore_signal(barrier, inc=1, device_id=peer, device_id_type=MESH)
    pl.semaphore_wait(barrier, len(peers))

    every = slice(None)
    pairs = (pl.ds(0, 2), pl.ds(2, 2))
    P_ = [(two, every, pl.ds(0, 128)) for two in pairs]
    Q_ = [(two, every, pl.ds(128, 128)) for two in pairs]

    def b_cols(s):
        return pl.ds(128, 384) if s < Q_FROM else pl.ds(256, 256)

    bz = recv_slots(18)
    pz, qz = [recv_slots(18) for _ in range(2)], [recv_slots(18) for _ in range(2)]
    p0 = recv_slots(4)
    w_own = pltpu.make_async_copy(w_ref, wbuf.at[0, x], load_sem.at[4])
    left, right, far = (x + 3) % NX, (x + 1) % NX, (x + 2) % NX
    rows1, rows2 = pl.ds(0, 32), pl.ds(32, 32)

    def w_begin():
        for d in (2, 1, 3):
            copy(w_ref.at[:, pl.ds(0, 128)], wbuf.at[0, x, :, pl.ds(0, 128)], p0 + d, at_x(d))
        copy(w_ref.at[:, b_cols(1)], wbuf.at[15, x, :, b_cols(1)], bz + 1, at_z(1))
        copy(w_ref.at[:, b_cols(1)], wbuf.at[1, x, :, b_cols(1)], bz + 9 + 1, at_z(NZ - 1))
        w_own.start()

    def z_send(s, region, slots, to_right, to_left):
        if to_right:
            copy(wbuf.at[((17 - s) % NZ,) + region], wbuf.at[(16 - s,) + region], slots + s, at_z(1))
        if to_left:
            copy(wbuf.at[(s - 1,) + region], wbuf.at[(s,) + region], slots + 9 + s, at_z(NZ - 1))

    def p_start():
        for d in (1, 3, 2):
            arrived(wbuf.at[0, (x + NX - d) % NX, every, pl.ds(0, 128)], p0 + d)
        for k in (0, 1):
            z_send(1, P_[k], pz[k], True, True)

    def p_step(s):
        for k in (0, 1):
            a_step(s, P_[k], pz[k])

    def q_start():
        for k in (0, 1):
            z_send(Q_FROM, Q_[k], qz[k], True, True)

    def q_step(s):
        for k in (0, 1):
            a_step(s, Q_[k], qz[k])

    def a_step(s, region, slots):
        arrived(wbuf.at[(16 - s,) + region], slots + s)
        if s < 8:
            z_send(s + 1, region, slots, True, False)
            arrived(wbuf.at[(s,) + region], slots + 9 + s)
            z_send(s + 1, region, slots, False, s < 7)

    def b_step(s):
        if s < 8:
            arrived(wbuf.at[16 - s, x, :, b_cols(s)], bz + s)
            z_send(s + 1, (x, every, b_cols(s + 1)), bz, s < 7, False)
        arrived(wbuf.at[s, x, :, b_cols(s)], bz + 9 + s)
        z_send(s + 1, (x, every, b_cols(s + 1)), bz, False, s < 8)

    slots_x = {}

    def b_spans(batch):
        lo, hi = batch[0], batch[-1]
        n = hi - lo + 1
        if lo == 0 or lo == 8:
            return [(pl.ds(lo, 1), batch)]
        return [(pl.ds(16 - hi, n), batch), (pl.ds(lo, n), batch)]

    def x_send(batch):
        cols = b_cols(batch[0])
        for k, (o, _) in enumerate(b_spans(batch)):
            base = slots_x[batch, k] = recv_slots(4)
            blk = wbuf.at[o, x, :, cols]
            copy(blk, blk, base + 0, at_x(1))
            copy(blk, blk, base + 1, at_x(3))

    def x_pass(batch):
        cols = b_cols(batch[0])
        for k, (o, _) in enumerate(b_spans(batch)):
            base = slots_x[batch, k]
            arrived(wbuf.at[o, left, :, cols], base + 0)
            blk = wbuf.at[o, left, rows1, cols]
            copy(blk, blk, base + 2, at_x(1))
            arrived(wbuf.at[o, right, :, cols], base + 1)
            blk = wbuf.at[o, right, rows2, cols]
            copy(blk, blk, base + 3, at_x(3))

    def x_end(batch):
        cols = b_cols(batch[0])
        for k, (o, _) in enumerate(b_spans(batch)):
            base = slots_x[batch, k]
            arrived(wbuf.at[o, far, rows1, cols], base + 2)
            arrived(wbuf.at[o, far, rows2, cols], base + 3)

    half = (pl.ds(0, 256), pl.ds(256, 256))
    iR, iL, iF, iS = recv_slots(2), recv_slots(2), recv_slots(2), recv_slots(8)

    def ihead(d):
        return ((y + d) % NY) * 2 + c

    i_own = pltpu.make_async_copy(inp_ref, inpb.at[head], load_sem.at[5])

    def input_begin():
        i_own.start()
        copy(inp_ref.at[:, half[0]], inpb.at[head, :, half[0]], iR + 0, at_y(1))
        copy(inp_ref.at[:, half[1]], inpb.at[head, :, half[1]], iL + 1, at_y(3))
        copy(inp_ref.at[:, half[1]], inpb.at[head, :, half[1]], iR + 1, at_y(1))
        copy(inp_ref.at[:, half[0]], inpb.at[head, :, half[0]], iL + 0, at_y(3))
        copy(inp_ref, inpb.at[head], iS + 0, sib)

    def input_pass(part):
        left, right, far = ihead(3), ihead(1), ihead(2)
        if part == 0:
            arrived(inpb.at[left, :, half[0]], iR + 0)
            copy(inpb.at[left, :, half[0]], inpb.at[left, :, half[0]], iF + 0, at_y(1))
            arrived(inpb.at[right, :, half[1]], iL + 1)
            copy(inpb.at[right, :, half[1]], inpb.at[right, :, half[1]], iF + 1, at_y(3))
            copy(inpb.at[left, :, half[0]], inpb.at[left, :, half[0]], iS + 1, sib)
            copy(inpb.at[right, :, half[1]], inpb.at[right, :, half[1]], iS + 2, sib)
        if part == 1:
            arrived(inpb.at[left, :, half[1]], iR + 1)
            copy(inpb.at[left, :, half[1]], inpb.at[left, :, half[1]], iS + 3, sib)
            arrived(inpb.at[right, :, half[0]], iL + 0)
            copy(inpb.at[right, :, half[0]], inpb.at[right, :, half[0]], iS + 4, sib)
        if part == 2:
            for k in (0, 1):
                arrived(inpb.at[far, :, half[k]], iF + k)
                copy(inpb.at[far, :, half[k]], inpb.at[far, :, half[k]], iS + 5 + k, sib)
        if part == 3:
            i_own.wait()

            def other(d):
                return ((y + d) % NY) * 2 + (1 - c)
            arrived(inpb.at[other(0)], iS + 0)
            arrived(inpb.at[other(3), :, half[0]], iS + 1)
            arrived(inpb.at[other(1), :, half[1]], iS + 2)
            arrived(inpb.at[other(3), :, half[1]], iS + 3)
            arrived(inpb.at[other(1), :, half[0]], iS + 4)
            for k in (0, 1):
                arrived(inpb.at[other(2), :, half[k]], iS + 5 + k)

    lane = iota((SPAN, 128), 1)
    low = lane < 64
    lowrow = iota((1, 128), 1) < 64
    ti, tj = iota((SPAN, SPAN), 0), iota((SPAN, SPAN), 1)
    upto = ti <= tj

    def pair(col, i):
        return jnp.where(low, col[:, 2 * i:2 * i + 1], col[:, 2 * i + 1:2 * i + 2])

    def pair_row(row, i):
        return jnp.where(lowrow, row[:, 2 * i:2 * i + 1], row[:, 2 * i + 1:2 * i + 2])

    def first(sp):
        rows = pl.ds(sp * SPAN, SPAN)
        rr = mm(ld_ref[:, rows], upto.astype(F32), EXACT)
        rc = jnp.concatenate([rr, jnp.zeros((120, SPAN), F32)], 0).T
        rr_ref[sp] = rr
        rc_ref[sp] = rc
        last = rc[SPAN - 1:SPAN, :]
        ec, tc, al = jnp.exp(rc), jnp.exp(last - rc), jnp.exp(last)
        ct = c_ref[rows, :].T
        for i in range(4):
            cols = pl.ds(i * 128, 128)
            v = (g_ref[rows, cols].astype(F32) * pair(ec, i)).astype(BF)
            v_ref[rows, cols] = v
            te_ref[rows, cols] = pair(tc, i)
            a_ref[sp, i] = jnp.broadcast_to(pair_row(al, i), (8, 128))
            gst[sp, i] = mm(ct, v)
        mt_ref[sp] = mm_nt(b_ref[rows, :], c_ref[rows, :])

    def unit1(sp, i):
        rows, cols = pl.ds(sp * SPAN, SPAN), pl.ds(i * 128, 128)
        g2 = g_ref[rows, cols]
        mt = mt_ref[sp]
        parts = []
        for k in (0, 1):
            h = 2 * i + k
            diff = rr_ref[sp, h:h + 1, :] - rc_ref[sp, :, h:h + 1]
            lt = jnp.exp(jnp.where(upto, diff, NEG))
            lt_ref[sp * 8 + h] = lt
            parts.append(mm((lt * mt).astype(BF), g2))
        skip = jnp.where(lowrow, sk_ref[2 * i], sk_ref[2 * i + 1])
        gxf[rows, cols] = jnp.where(low, parts[0], parts[1]) + skip * g2.astype(F32)

    def scan_x_send(which, state):
        base = recv_slots(4)
        for i in range(4):
            sx_ref[which, i] = state(i).astype(BF)
        for d in (1, 3, 2):
            to = (x + d) % NX
            copy(sx_ref.at[which, to], xr.at[which, x], base + d, at_x(d))
        xr[which, x] = sx_ref[which, x]
        return base

    def scan_x_wait(which, base):
        for d in (1, 2, 3):
            arrived(xr.at[which, (x + NX - d) % NX], base + d)

    def scan_z_send(which):
        base = recv_slots(16)
        for d in FAR_FIRST:
            to = (z + d) % NZ
            copy(tz.at[which, to], zr.at[which, z], base + d, at_z(d))
        zr[which, z] = tz[which, z]
        return base

    def scan_z_wait(which, base):
        for d in range(1, NZ):
            arrived(zr.at[which, (z + NZ - d) % NZ], base + d)

    def scan_z_back(which):
        base = recv_slots(16)
        for d in FAR_FIRST:
            to = (z + d) % NZ
            copy(zo.at[which, to], zp.at[which, z], base + d, at_z(d))
        zp[which, z] = zo[which, z]
        return base

    def scan_z_back_wait(which, base):
        for d in range(1, NZ):
            arrived(zp.at[which, (z + NZ - d) % NZ], base + d)

    def scan_x_back(which):
        base = recv_slots(4)
        for d in (1, 3, 2):
            to = (x + d) % NX
            copy(bo_ref.at[which, to], br_ref.at[which, x], base + d, at_x(d))
        br_ref[which, x] = bo_ref[which, x]
        return base

    def scan_x_back_wait(which, base):
        for d in (1, 2, 3):
            arrived(br_ref.at[which, (x + NX - d) % NX], base + d)

    marks = {}

    def ret_x():
        base = recv_slots(4)
        for i in range(4):
            adev[i] = a_ref[0, i] * a_ref[1, i]
        for d in (1, 3, 2):
            to = (x + d) % NX
            copy(adev.at[to], ax_ref.at[x], base + d, at_x(d))
        ax_ref[x] = adev[x]
        marks["ax"] = base

    def ret_z():
        for d in (1, 2, 3):
            arrived(ax_ref.at[(x + NX - d) % NX], marks["ax"] + d)
        base = recv_slots(16)
        adev[4] = ax_ref[0] * ax_ref[1] * ax_ref[2] * ax_ref[3]
        for d in FAR_FIRST:
            copy(adev.at[4], az_ref.at[z], base + d, at_z(d))
        az_ref[z] = adev[4]
        marks["az"] = base

    def ret_wait():
        for d in range(1, NZ):
            arrived(az_ref.at[(z + NZ - d) % NZ], marks["az"] + d)

    def ret(k):
        return ax_ref[k][0:1, :]

    def put_total(which, total):
        for k in range(NZ):
            tz[which, k] = total[8 * k:8 * k + 8, :]

    def bscan(part):
        if part == 0:
            marks["b0"] = scan_x_send(0, lambda i: gst[0, i] + a_ref[0, i][0:1, :] * gst[1, i])
        if part == 1:
            scan_x_wait(0, marks["b0"])
            total = xr[0, 3].astype(F32)
            for k in (2, 1, 0):
                total = xr[0, k].astype(F32) + ret(k) * total
            put_total(0, total)
            marks["b1"] = scan_z_send(0)
        if part == 2:
            ret_wait()
            scan_z_wait(0, marks["b1"])
            q = jnp.zeros((8, 128), F32)
            for k in range(NZ - 1, -1, -1):
                zo[0, k] = q
                q = zr[0, k] + az_ref[k] * q
            marks["b2"] = scan_z_back(0)
        if part == 3:
            scan_z_back_wait(0, marks["b2"])
            q = jnp.concatenate([zp[0, k] for k in range(NZ)], 0)
            for k in (3, 2, 1, 0):
                bo_ref[0, k] = q.astype(BF)
                if k:
                    q = xr[0, k].astype(F32) + ret(k) * q
            marks["b3"] = scan_x_back(0)
        if part == 4:
            scan_x_back_wait(0, marks["b3"])
            for i in range(4):
                cols = pl.ds(i * 128, 128)
                q = br_ref[0, i]
                qs[1, :, cols] = q
                qs[0, :, cols] = (gst[1, i] + a_ref[1, i][0:1, :] * q.astype(F32)).astype(BF)

    def fscan(part):
        if part == 0:
            marks["f0"] = scan_x_send(1, lambda i: a_ref[1, i][0:1, :] * est[0, i] + est[1, i])
        if part == 1:
            scan_x_wait(1, marks["f0"])
            total = xr[1, 0].astype(F32)
            for k in (1, 2, 3):
                total = xr[1, k].astype(F32) + ret(k) * total
            put_total(1, total)
            marks["f1"] = scan_z_send(1)
        if part == 2:
            scan_z_wait(1, marks["f1"])
            s = jnp.zeros((8, 128), F32)
            for k in range(NZ):
                zo[1, k] = s
                s = zr[1, k] + az_ref[k] * s
            marks["f2"] = scan_z_back(1)
        if part == 3:
            scan_z_back_wait(1, marks["f2"])
            s = jnp.concatenate([zp[1, k] for k in range(NZ)], 0)
            for k in range(NX):
                bo_ref[1, k] = s.astype(BF)
                if k < NX - 1:
                    s = xr[1, k].astype(F32) + ret(k) * s
            marks["f3"] = scan_x_back(1)
        if part == 4:
            scan_x_back_wait(1, marks["f3"])
            for i in range(4):
                cols = pl.ds(i * 128, 128)
                s = br_ref[1, i]
                ss[0, :, cols] = s
                ss[1, :, cols] = (a_ref[0, i][0:1, :] * s.astype(F32) + est[0, i]).astype(BF)

    def finish_gx(sp):
        rows = pl.ds(sp * SPAN, SPAN)
        gx[rows, :] = (gxf[rows, :] + te_ref[rows, :] * mm(b_ref[rows, :], qs[sp])).astype(BF)

    def project(first_o, count):
        def one(k, carry):
            o = (first_o + k) % NZ
            zz = (z + o) % NZ
            cols = pl.ds(pl.multiple_of((zz % 2) * 256, 256), 256)
            xacc[...] += mm(inpb[zz // 2, :, cols], wbuf[o].reshape(256, 512))
            return carry

        lax.fori_loop(0, count, one, 0)

    def own_states():
        xb = xacc[...].astype(BF)
        x_ref[...] = xb
        ex_ref[...] = (te_ref[...] * xb.astype(F32)).astype(BF)
        for sp in range(2):
            rows = pl.ds(sp * SPAN, SPAN)
            bt = b_ref[rows, :].T
            for i in range(4):
                est[sp, i] = mm(bt, ex_ref[rows, pl.ds(i * 128, 128)])

    rS = recv_slots(4)

    def part_of(j, k):
        return mm_nt(gx[...], wbuf[(2 * j + k + NZ - z) % NZ].reshape(256, 512))

    def rs_sib():
        for d in (2, 1, 3, 0):
            j = ((y + d) % NY) * 2 + (1 - c)
            for k in (0, 1):
                pbuf[j, :, half[k]] = part_of(j, k).astype(BF)
            copy(pbuf.at[j], sibr.at[(y + d) % NY], rS + d, sib)

    rF, rN = recv_slots(2), recv_slots(4)

    def rs_own(d):
        yy = (y + d) % NY
        j = yy * 2 + c
        arrived(sibr.at[yy], rS + d)
        for k in (0, 1):
            pbuf[j, :, half[k]] = (part_of(j, k) + sibr[yy, :, half[k]].astype(F32)).astype(BF)
        if d == 2:
            copy(pbuf.at[j, :, half[1]], yfar.at[:, half[1]], rF + 1, at_y(1))
            copy(pbuf.at[j, :, half[0]], yfar.at[:, half[0]], rF + 0, at_y(3))
        if d == 1:
            copy(pbuf.at[j, :, half[0]], ynear.at[0, :, half[0]], rN + 0, at_y(1))
        if d == 3:
            copy(pbuf.at[j, :, half[1]], ynear.at[1, :, half[1]], rN + 1, at_y(3))

    def rs_pass():
        j = ((y + 1) % NY) * 2 + c
        arrived(yfar.at[:, half[1]], rF + 1)
        pbuf[j, :, 256:512] = (pbuf[j, :, 256:512].astype(F32) + yfar[:, 256:512].astype(F32)).astype(BF)
        copy(pbuf.at[j, :, half[1]], ynear.at[0, :, half[1]], rN + 2, at_y(1))
        j = ((y + 3) % NY) * 2 + c
        arrived(yfar.at[:, half[0]], rF + 0)
        pbuf[j, :, 0:256] = (pbuf[j, :, 0:256].astype(F32) + yfar[:, 0:256].astype(F32)).astype(BF)
        copy(pbuf.at[j, :, half[0]], ynear.at[1, :, half[0]], rN + 3, at_y(3))

    def rs_end():
        arrived(ynear.at[0, :, half[0]], rN + 0)
        arrived(ynear.at[1, :, half[1]], rN + 1)
        arrived(ynear.at[0, :, half[1]], rN + 2)
        arrived(ynear.at[1, :, half[0]], rN + 3)
        gi_ref[...] = (
            pbuf[head].astype(F32) + ynear[0].astype(F32) + ynear[1].astype(F32)
        ).astype(BF)

    def unit2(sp):
        rows = pl.ds(sp * SPAN, SPAN)
        dmt[sp] = jnp.zeros((SPAN, SPAN), F32)
        dcol[sp] = jnp.zeros((SPAN, 128), F32)

        def one(i, carry):
            cols = pl.ds(pl.multiple_of(i * 128, 128), 128)
            g2, x2 = g_ref[rows, cols], x_ref[rows, cols]
            mt = mt_ref[sp]
            for k in (0, 1):
                h = 2 * i + k
                xm = jnp.where(low if k == 0 else jnp.logical_not(low), x2, jnp.zeros_like(x2))
                p = mm_nt(xm, g2) * lt_ref[sp * 8 + h]
                dmt[sp] += p
                wm = p * mt
                drow[sp, pl.ds(h, 1), :] = jnp.sum(wm, axis=0, keepdims=True)
                dcol[sp] += jnp.where(lane == h, jnp.sum(wm, axis=1, keepdims=True), 0.0)
            return carry

        lax.fori_loop(0, 4, one, 0)

    ind = (iota((8, 512), 1) // 64 == iota((8, 512), 0)).astype(BF)

    def head_sums(value):
        hi = value.astype(BF)
        lo = (value - hi.astype(F32)).astype(BF)
        return mm_nt(ind, hi) + mm_nt(ind, lo)

    def grad_b_part(sp):
        rows = pl.ds(sp * SPAN, SPAN)
        pr[0, rows, :] = (mm(dmt[sp].astype(BF), c_ref[rows, :]) + mm_nt(ex_ref[rows, :], qs[sp])).astype(BF)

    def grad_c_part(sp):
        rows = pl.ds(sp * SPAN, SPAN)
        pr[1, rows, :] = (
            mm_tn(dmt[sp].astype(BF), b_ref[rows, :]) + mm_nt(v_ref[rows, :], ss[sp])
        ).astype(BF)

    def decay_part(sp):
        rows = pl.ds(sp * SPAN, SPAN)
        u = mm(c_ref[rows, :], ss[sp])
        arow = jnp.concatenate([a_ref[sp, i][0:1, :] for i in range(4)], 1)
        cross = jnp.sum(qs[sp].astype(F32) * ss[sp].astype(F32), axis=0, keepdims=True) * arow
        is_last = iota((SPAN, 512), 0) == SPAN - 1
        vv = v_ref[rows, :].astype(F32) * u + jnp.where(is_last, cross, 0.0)
        tt = te_ref[rows, :] * x_ref[rows, :].astype(F32) * mm(b_ref[rows, :], qs[sp])
        dr = head_sums(vv) + drow[sp] - dcol[sp].T[0:8, :]
        gld_ref[:, rows] = mm(dr, (ti >= tj).astype(F32), EXACT) + mm(head_sums(tt), (ti < tj).astype(F32), EXACT)

    def mine(k):
        return pl.ds(pl.multiple_of(k * 64, 64), 64)

    def ps_send(which):
        base = recv_slots(8)
        for d in range(1, 8):
            to = (head + d) % 8
            copy(pr.at[which, mine(to), :], prr.at[which, head], base + d, at_head(d))
        prr[which, head] = pr[which, mine(head), :]
        return base

    def ps_sum(which, base):
        for d in range(1, 8):
            arrived(prr.at[which, (head + 8 - d) % 8], base + d)
        total = prr[which, 0].astype(F32)
        for k in range(1, 8):
            total = total + prr[which, k].astype(F32)
        pfin[which] = total.astype(BF)
        base = recv_slots(8)
        for d in range(1, 8):
            copy(pfin.at[which], pfull.at[which, mine(head), :], base + d, at_head(d))
        pfull[which, mine(head), :] = pfin[which]
        return base

    def ps_end(which, base, out):
        for d in range(1, 8):
            arrived(pfull.at[which, mine((head + 8 - d) % 8), :], base + d)
        out[...] = pfull[which].astype(F32)

    stores = []

    def put(src, dst):
        d = pltpu.make_async_copy(src, dst, load_sem.at[6 + len(stores)])
        d.start()
        stores.append(d)

    w_begin()
    input_begin()
    for d in loads:
        d.wait()
    w_own.wait()
    x_send((0,))
    first(0)
    p_start()
    b_step(1)
    first(1)
    ret_x()
    bscan(0)
    b_step(2)
    x_send((1, 2))
    xacc[...] = jnp.zeros_like(xacc)
    p_step(1)
    unit1(0, 0)
    b_step(3)
    x_send((3,))
    x_pass((0,))
    p_step(2)
    unit1(0, 1)
    b_step(4)
    x_pass((1, 2))
    x_end((0,))
    ret_z()
    bscan(1)
    input_pass(0)
    x_pass((3,))
    p_step(3)
    unit1(0, 2)
    b_step(5)
    x_send((4, 5))
    x_end((1, 2))
    x_end((3,))
    q_start()
    p_step(4)
    unit1(0, 3)
    b_step(6)
    x_send((6,))
    x_pass((4, 5))
    q_step(4)
    bscan(2)
    input_pass(1)
    p_step(5)
    unit1(1, 0)
    b_step(7)
    x_send((7,))
    x_pass((6,))
    q_step(5)
    p_step(6)
    unit1(1, 1)
    b_step(8)
    x_send((8,))
    x_end((4, 5))
    x_pass((7,))
    q_step(6)
    bscan(3)
    input_pass(2)
    p_step(7)
    unit1(1, 2)
    x_end((6,))
    x_pass((8,))
    q_step(7)
    unit1(1, 3)
    input_pass(3)
    project(NZ - 6, 13)
    p_step(8)
    x_end((7,))
    x_end((8,))
    q_step(8)
    project(7, 3)
    bscan(4)
    finish_gx(0)
    finish_gx(1)
    own_states()
    fscan(0)
    rs_sib()
    rs_own(2)
    fscan(1)
    rs_own(1)
    rs_own(3)
    rs_own(0)
    unit2(0)
    fscan(2)
    unit2(1)
    rs_pass()
    grad_b_part(0)
    grad_b_part(1)
    pb = ps_send(0)
    fscan(3)
    pb = ps_sum(0, pb)
    fscan(4)
    grad_c_part(0)
    grad_c_part(1)
    pc = ps_send(1)
    decay_part(0)
    pc = ps_sum(1, pc)
    decay_part(1)
    put(gld_ref, gld_hbm)
    ps_end(0, pb, gb_ref)
    put(gb_ref, gb_hbm)
    rs_end()
    put(gi_ref, gi_hbm)
    ps_end(1, pc, gc_ref)
    put(gc_ref, gc_hbm)
    for d in stores:
        d.wait()
    for d in sent:
        d.wait_send()
    assert counts["s"] <= N_SEND and counts["r"] <= N_RECV, counts


def local(inputs, w_in, b_rows, c_rows, log_decay, skip_gain, grad_out):
    hbm = pl.BlockSpec(memory_space=pl.ANY)
    V = pltpu.VMEM
    return pl.pallas_call(
        kernel,
        out_shape=(
            jax.ShapeDtypeStruct((T, 512), BF),
            jax.ShapeDtypeStruct((T, 128), F32),
            jax.ShapeDtypeStruct((T, 128), F32),
            jax.ShapeDtypeStruct((8, T), F32),
        ),
        in_specs=[hbm] * 5 + [pl.BlockSpec(memory_space=pltpu.SMEM), hbm],
        out_specs=(hbm,) * 4,
        scratch_shapes=[
            V((T, 128), BF),
            V((T, 128), BF),
            V((8, T), F32),
            V((T, 512), BF),
            V((T, 512), BF),
            V((T, 128), F32),
            V((T, 128), F32),
            V((8, T), F32),
            V((NZ, NX, 64, 512), BF),
            V((8, T, 512), BF),
            V((8, T, 512), BF),
            V((4, T, 512), BF),
            V((T, 512), BF),
            V((2, T, 512), BF),
            V((16, SPAN, SPAN), F32),
            V((2, SPAN, SPAN), F32),
            V((T, 512), F32),
            V((T, 512), BF),
            V((T, 512), F32),
            V((T, 512), BF),
            V((T, 512), F32),
            V((T, 512), BF),
            V((T, 512), BF),
            V((2, 8, SPAN), F32),
            V((2, SPAN, 128), F32),
            V((2, 4, 8, 128), F32),
            V((5, 8, 128), F32),
            V((4, 8, 128), F32),
            V((16, 8, 128), F32),
            V((2, 4, 128, 128), F32),
            V((2, 4, 128, 128), F32),
            V((2, 128, 512), BF),
            V((2, 128, 512), BF),
            V((2, 4, 128, 128), BF),
            V((2, 4, 128, 128), BF),
            V((2, 16, 8, 128), F32),
            V((2, 16, 8, 128), F32),
            V((2, 16, 8, 128), F32),
            V((2, 16, 8, 128), F32),
            V((2, 4, 128, 128), BF),
            V((2, 4, 128, 128), BF),
            V((2, SPAN, SPAN), F32),
            V((2, 8, SPAN), F32),
            V((2, SPAN, 128), F32),
            V((2, T, 128), BF),
            V((2, 8, 64, 128), BF),
            V((2, 64, 128), BF),
            V((2, T, 128), BF),
            pltpu.SemaphoreType.DMA((N_SEND,)),
            pltpu.SemaphoreType.DMA((N_RECV,)),
            pltpu.SemaphoreType.DMA((10,)),
        ],
        compiler_params=pltpu.CompilerParams(
            collective_id=0, has_side_effects=True, vmem_limit_bytes=60 * 1024 * 1024
        ),
        cost_estimate=pl.CostEstimate(flops=8 * 10**9, bytes_accessed=4 * 10**6, transcendentals=2 * 10**6),
    )(inputs, w_in, b_rows, c_rows, log_decay, skip_gain, grad_out)


def solution(mesh):
    in_specs = (
        P("ctx", "head"),
        P("ctx", "head"),
        P("ctx", None),
        P("ctx", None),
        P("head", "ctx"),
        P("head"),
        P("ctx", "head"),
    )
    out_specs = (P("ctx", "head"), P("ctx", None), P("ctx", None), P("head", "ctx"))
    return jax.shard_map(local, mesh=mesh, in_specs=in_specs, out_specs=out_specs, check_vma=False)
```

```python
import jax
import jax.numpy as jnp
from jax import lax
from jax.experimental import pallas as pl
from jax.experimental.pallas import tpu as pltpu
from jax.sharding import PartitionSpec as P

MESH = pl.DeviceIdType.MESH
BF = jnp.bfloat16
F32 = jnp.float32
EXACT = lax.Precision.HIGHEST
NX, NY, NZ = 4, 4, 16
SPAN = 256
T = 512
NEG = -1e30
Q_FROM = 4
FAR_FIRST = sorted(range(1, NZ), key=lambda d: -min(d, NZ - d))


def mm(a, b, precision=None):
    return lax.dot_general(a, b, (((1,), (0,)), ((), ())), precision=precision, preferred_element_type=F32)


def mm_nt(a, b, precision=None):
    return lax.dot_general(a, b, (((1,), (1,)), ((), ())), precision=precision, preferred_element_type=F32)


def mm_tn(a, b):
    return lax.dot_general(a, b, (((0,), (0,)), ((), ())), preferred_element_type=F32)


def iota(shape, dim):
    return lax.broadcasted_iota(jnp.int32, shape, dim)


N_SEND = 300
N_RECV = 340


def kernel(
    inp_ref, w_ref, b_hbm, c_hbm, ld_hbm, sk_ref, g_hbm,
    gi_hbm, gb_hbm, gc_hbm, gld_hbm,
    b_ref, c_ref, ld_ref, g_ref, gi_ref, gb_ref, gc_ref, gld_ref,
    wbuf, inpb, pbuf, sibr, yfar, ynear, lt_ref, mt_ref, gxf, gx, te_ref, v_ref, xacc, x_ref, ex_ref,
    rr_ref, rc_ref, a_ref, adev, ax_ref, az_ref,
    gst, est, qs, ss, sx_ref, xr, tz, zr, zo, zp, bo_ref, br_ref,
    dmt, drow, dcol, pr, prr, pfin, pfull,
    send_sem, recv_sem, load_sem,
):
    ctx = lax.axis_index("ctx")
    head = lax.axis_index("head")
    z, x = ctx // NX, ctx % NX
    y, c = head // 2, head % 2

    def at_x(d):
        return (z * NX + (x + d) % NX, head)

    def at_z(d):
        return (((z + d) % NZ) * NX + x, head)

    def at_y(d):
        return (ctx, ((y + d) % NY) * 2 + c)

    sib = (ctx, y * 2 + (1 - c))

    def at_head(d):
        return (ctx, (head + d) % 8)

    counts = {"s": 0, "r": 0}
    sent = []

    def recv_slots(n):
        base = counts["r"]
        counts["r"] += n
        return base

    def copy(src, dst, slot, device):
        k = counts["s"]
        counts["s"] += 1
        d = pltpu.make_async_remote_copy(
            src_ref=src, dst_ref=dst, send_sem=send_sem.at[k], recv_sem=recv_sem.at[slot],
            device_id=device, device_id_type=MESH,
        )
        d.start()
        sent.append(d)

    def arrived(dst, slot):
        pltpu.make_async_remote_copy(
            src_ref=dst, dst_ref=dst, send_sem=send_sem.at[0], recv_sem=recv_sem.at[slot],
            device_id=sib, device_id_type=MESH,
        ).wait_recv()

    loads = []
    for src, dst in ((ld_hbm, ld_ref), (c_hbm, c_ref), (g_hbm, g_ref), (b_hbm, b_ref)):
        d = pltpu.make_async_copy(src, dst, load_sem.at[len(loads)])
        d.start()
        loads.append(d)

    barrier = pltpu.get_barrier_semaphore()
    peers = [at_x(d) for d in range(1, NX)] + [at_z(d) for d in range(1, NZ)] + [at_head(d) for d in range(1, 8)]
    for peer in peers:
        pl.semaphore_signal(barrier, inc=1, device_id=peer, device_id_type=MESH)
    pl.semaphore_wait(barrier, len(peers))

    every = slice(None)
    pairs = (pl.ds(0, 2), pl.ds(2, 2))
    P_ = [(two, every, pl.ds(0, 128)) for two in pairs]
    Q_ = [(two, every, pl.ds(128, 128)) for two in pairs]

    def b_cols(s):
        return pl.ds(128, 384) if s < Q_FROM else pl.ds(256, 256)

    bz = recv_slots(18)
    pz, qz = [recv_slots(18) for _ in range(2)], [recv_slots(18) for _ in range(2)]
    p0 = recv_slots(4)
    w_own = pltpu.make_async_copy(w_ref, wbuf.at[0, x], load_sem.at[4])
    left, right, far = (x + 3) % NX, (x + 1) % NX, (x + 2) % NX
    rows1, rows2 = pl.ds(0, 32), pl.ds(32, 32)

    def w_begin():
        for d in (2, 1, 3):
            copy(w_ref.at[:, pl.ds(0, 128)], wbuf.at[0, x, :, pl.ds(0, 128)], p0 + d, at_x(d))
        copy(w_ref.at[:, b_cols(1)], wbuf.at[15, x, :, b_cols(1)], bz + 1, at_z(1))
        copy(w_ref.at[:, b_cols(1)], wbuf.at[1, x, :, b_cols(1)], bz + 9 + 1, at_z(NZ - 1))
        w_own.start()

    def z_send(s, region, slots, to_right, to_left):
        if to_right:
            copy(wbuf.at[((17 - s) % NZ,) + region], wbuf.at[(16 - s,) + region], slots + s, at_z(1))
        if to_left:
            copy(wbuf.at[(s - 1,) + region], wbuf.at[(s,) + region], slots + 9 + s, at_z(NZ - 1))

    def p_start():
        for d in (1, 3, 2):
            arrived(wbuf.at[0, (x + NX - d) % NX, every, pl.ds(0, 128)], p0 + d)
        for k in (0, 1):
            z_send(1, P_[k], pz[k], True, True)

    def p_step(s):
        for k in (0, 1):
            a_step(s, P_[k], pz[k])

    def q_start():
        for k in (0, 1):
            z_send(Q_FROM, Q_[k], qz[k], True, True)

    def q_step(s):
        for k in (0, 1):
            a_step(s, Q_[k], qz[k])

    def a_step(s, region, slots):
        arrived(wbuf.at[(16 - s,) + region], slots + s)
        if s < 8:
            z_send(s + 1, region, slots, True, False)
            arrived(wbuf.at[(s,) + region], slots + 9 + s)
            z_send(s + 1, region, slots, False, s < 7)

    def b_step(s):
        if s < 8:
            arrived(wbuf.at[16 - s, x, :, b_cols(s)], bz + s)
            z_send(s + 1, (x, every, b_cols(s + 1)), bz, s < 7, False)
        arrived(wbuf.at[s, x, :, b_cols(s)], bz + 9 + s)
        z_send(s + 1, (x, every, b_cols(s + 1)), bz, False, s < 8)

    slots_x = {}

    def b_spans(batch):
        lo, hi = batch[0], batch[-1]
        n = hi - lo + 1
        if lo == 0 or lo == 8:
            return [(pl.ds(lo, 1), batch)]
        return [(pl.ds(16 - hi, n), batch), (pl.ds(lo, n), batch)]

    def x_send(batch):
        cols = b_cols(batch[0])
        for k, (o, _) in enumerate(b_spans(batch)):
            base = slots_x[batch, k] = recv_slots(4)
            blk = wbuf.at[o, x, :, cols]
            copy(blk, blk, base + 0, at_x(1))
            copy(blk, blk, base + 1, at_x(3))

    def x_pass(batch):
        cols = b_cols(batch[0])
        for k, (o, _) in enumerate(b_spans(batch)):
            base = slots_x[batch, k]
            arrived(wbuf.at[o, left, :, cols], base + 0)
            blk = wbuf.at[o, left, rows1, cols]
            copy(blk, blk, base + 2, at_x(1))
            arrived(wbuf.at[o, right, :, cols], base + 1)
            blk = wbuf.at[o, right, rows2, cols]
            copy(blk, blk, base + 3, at_x(3))

    def x_end(batch):
        cols = b_cols(batch[0])
        for k, (o, _) in enumerate(b_spans(batch)):
            base = slots_x[batch, k]
            arrived(wbuf.at[o, far, rows1, cols], base + 2)
            arrived(wbuf.at[o, far, rows2, cols], base + 3)

    half = (pl.ds(0, 256), pl.ds(256, 256))
    iR, iL, iF, iS = recv_slots(2), recv_slots(2), recv_slots(2), recv_slots(8)

    def ihead(d):
        return ((y + d) % NY) * 2 + c

    i_own = pltpu.make_async_copy(inp_ref, inpb.at[head], load_sem.at[5])

    def input_begin():
        i_own.start()
        copy(inp_ref.at[:, half[0]], inpb.at[head, :, half[0]], iR + 0, at_y(1))
        copy(inp_ref.at[:, half[1]], inpb.at[head, :, half[1]], iL + 1, at_y(3))
        copy(inp_ref.at[:, half[1]], inpb.at[head, :, half[1]], iR + 1, at_y(1))
        copy(inp_ref.at[:, half[0]], inpb.at[head, :, half[0]], iL + 0, at_y(3))
        copy(inp_ref, inpb.at[head], iS + 0, sib)

    def input_pass(part):
        left, right, far = ihead(3), ihead(1), ihead(2)
        if part == 0:
            arrived(inpb.at[left, :, half[0]], iR + 0)
            copy(inpb.at[left, :, half[0]], inpb.at[left, :, half[0]], iF + 0, at_y(1))
            arrived(inpb.at[right, :, half[1]], iL + 1)
            copy(inpb.at[right, :, half[1]], inpb.at[right, :, half[1]], iF + 1, at_y(3))
            copy(inpb.at[left, :, half[0]], inpb.at[left, :, half[0]], iS + 1, sib)
            copy(inpb.at[right, :, half[1]], inpb.at[right, :, half[1]], iS + 2, sib)
        if part == 1:
            arrived(inpb.at[left, :, half[1]], iR + 1)
            copy(inpb.at[left, :, half[1]], inpb.at[left, :, half[1]], iS + 3, sib)
            arrived(inpb.at[right, :, half[0]], iL + 0)
            copy(inpb.at[right, :, half[0]], inpb.at[right, :, half[0]], iS + 4, sib)
        if part == 2:
            for k in (0, 1):
                arrived(inpb.at[far, :, half[k]], iF + k)
                copy(inpb.at[far, :, half[k]], inpb.at[far, :, half[k]], iS + 5 + k, sib)
        if part == 3:
            i_own.wait()

            def other(d):
                return ((y + d) % NY) * 2 + (1 - c)
            arrived(inpb.at[other(0)], iS + 0)
            arrived(inpb.at[other(3), :, half[0]], iS + 1)
            arrived(inpb.at[other(1), :, half[1]], iS + 2)
            arrived(inpb.at[other(3), :, half[1]], iS + 3)
            arrived(inpb.at[other(1), :, half[0]], iS + 4)
            for k in (0, 1):
                arrived(inpb.at[other(2), :, half[k]], iS + 5 + k)

    lane = iota((SPAN, 128), 1)
    low = lane < 64
    lowrow = iota((1, 128), 1) < 64
    ti, tj = iota((SPAN, SPAN), 0), iota((SPAN, SPAN), 1)
    upto = ti <= tj

    def pair(col, i):
        return jnp.where(low, col[:, 2 * i:2 * i + 1], col[:, 2 * i + 1:2 * i + 2])

    def pair_row(row, i):
        return jnp.where(lowrow, row[:, 2 * i:2 * i + 1], row[:, 2 * i + 1:2 * i + 2])

    def first(sp):
        rows = pl.ds(sp * SPAN, SPAN)
        rr = mm(ld_ref[:, rows], upto.astype(F32), EXACT)
        rc = jnp.concatenate([rr, jnp.zeros((120, SPAN), F32)], 0).T
        rr_ref[sp] = rr
        rc_ref[sp] = rc
        last = rc[SPAN - 1:SPAN, :]
        ec, tc, al = jnp.exp(rc), jnp.exp(last - rc), jnp.exp(last)
        ct = c_ref[rows, :].T
        for i in range(4):
            cols = pl.ds(i * 128, 128)
            v = (g_ref[rows, cols].astype(F32) * pair(ec, i)).astype(BF)
            v_ref[rows, cols] = v
            te_ref[rows, cols] = pair(tc, i)
            a_ref[sp, i] = jnp.broadcast_to(pair_row(al, i), (8, 128))
            gst[sp, i] = mm(ct, v)
        mt_ref[sp] = mm_nt(b_ref[rows, :], c_ref[rows, :])

    def unit1(sp, i):
        rows, cols = pl.ds(sp * SPAN, SPAN), pl.ds(i * 128, 128)
        g2 = g_ref[rows, cols]
        mt = mt_ref[sp]
        parts = []
        for k in (0, 1):
            h = 2 * i + k
            diff = rr_ref[sp, h:h + 1, :] - rc_ref[sp, :, h:h + 1]
            lt = jnp.exp(jnp.where(upto, diff, NEG))
            lt_ref[sp * 8 + h] = lt
            parts.append(mm((lt * mt).astype(BF), g2))
        skip = jnp.where(lowrow, sk_ref[2 * i], sk_ref[2 * i + 1])
        gxf[rows, cols] = jnp.where(low, parts[0], parts[1]) + skip * g2.astype(F32)

    def scan_x_send(which, state):
        base = recv_slots(4)
        for i in range(4):
            sx_ref[which, i] = state(i).astype(BF)
        for d in (1, 3, 2):
            to = (x + d) % NX
            copy(sx_ref.at[which, to], xr.at[which, x], base + d, at_x(d))
        xr[which, x] = sx_ref[which, x]
        return base

    def scan_x_wait(which, base):
        for d in (1, 2, 3):
            arrived(xr.at[which, (x + NX - d) % NX], base + d)

    def scan_z_send(which):
        base = recv_slots(16)
        for d in FAR_FIRST:
            to = (z + d) % NZ
            copy(tz.at[which, to], zr.at[which, z], base + d, at_z(d))
        zr[which, z] = tz[which, z]
        return base

    def scan_z_wait(which, base):
        for d in range(1, NZ):
            arrived(zr.at[which, (z + NZ - d) % NZ], base + d)

    def scan_z_back(which):
        base = recv_slots(16)
        for d in FAR_FIRST:
            to = (z + d) % NZ
            copy(zo.at[which, to], zp.at[which, z], base + d, at_z(d))
        zp[which, z] = zo[which, z]
        return base

    def scan_z_back_wait(which, base):
        for d in range(1, NZ):
            arrived(zp.at[which, (z + NZ - d) % NZ], base + d)

    def scan_x_back(which):
        base = recv_slots(4)
        for d in (1, 3, 2):
            to = (x + d) % NX
            copy(bo_ref.at[which, to], br_ref.at[which, x], base + d, at_x(d))
        br_ref[which, x] = bo_ref[which, x]
        return base

    def scan_x_back_wait(which, base):
        for d in (1, 2, 3):
            arrived(br_ref.at[which, (x + NX - d) % NX], base + d)

    marks = {}

    def ret_x():
        base = recv_slots(4)
        for i in range(4):
            adev[i] = a_ref[0, i] * a_ref[1, i]
        for d in (1, 3, 2):
            to = (x + d) % NX
            copy(adev.at[to], ax_ref.at[x], base + d, at_x(d))
        ax_ref[x] = adev[x]
        marks["ax"] = base

    def ret_z():
        for d in (1, 2, 3):
            arrived(ax_ref.at[(x + NX - d) % NX], marks["ax"] + d)
        base = recv_slots(16)
        adev[4] = ax_ref[0] * ax_ref[1] * ax_ref[2] * ax_ref[3]
        for d in FAR_FIRST:
            copy(adev.at[4], az_ref.at[z], base + d, at_z(d))
        az_ref[z] = adev[4]
        marks["az"] = base

    def ret_wait():
        for d in range(1, NZ):
            arrived(az_ref.at[(z + NZ - d) % NZ], marks["az"] + d)

    def ret(k):
        return ax_ref[k][0:1, :]

    def put_total(which, total):
        for k in range(NZ):
            tz[which, k] = total[8 * k:8 * k + 8, :]

    def bscan(part):
        if part == 0:
            marks["b0"] = scan_x_send(0, lambda i: gst[0, i] + a_ref[0, i][0:1, :] * gst[1, i])
        if part == 1:
            scan_x_wait(0, marks["b0"])
            total = xr[0, 3].astype(F32)
            for k in (2, 1, 0):
                total = xr[0, k].astype(F32) + ret(k) * total
            put_total(0, total)
            marks["b1"] = scan_z_send(0)
        if part == 2:
            ret_wait()
            scan_z_wait(0, marks["b1"])
            q = jnp.zeros((8, 128), F32)
            for k in range(NZ - 1, -1, -1):
                zo[0, k] = q
                q = zr[0, k] + az_ref[k] * q
            marks["b2"] = scan_z_back(0)
        if part == 3:
            scan_z_back_wait(0, marks["b2"])
            q = jnp.concatenate([zp[0, k] for k in range(NZ)], 0)
            for k in (3, 2, 1, 0):
                bo_ref[0, k] = q.astype(BF)
                if k:
                    q = xr[0, k].astype(F32) + ret(k) * q
            marks["b3"] = scan_x_back(0)
        if part == 4:
            scan_x_back_wait(0, marks["b3"])
            for i in range(4):
                cols = pl.ds(i * 128, 128)
                q = br_ref[0, i]
                qs[1, :, cols] = q
                qs[0, :, cols] = (gst[1, i] + a_ref[1, i][0:1, :] * q.astype(F32)).astype(BF)

    def fscan(part):
        if part == 0:
            marks["f0"] = scan_x_send(1, lambda i: a_ref[1, i][0:1, :] * est[0, i] + est[1, i])
        if part == 1:
            scan_x_wait(1, marks["f0"])
            total = xr[1, 0].astype(F32)
            for k in (1, 2, 3):
                total = xr[1, k].astype(F32) + ret(k) * total
            put_total(1, total)
            marks["f1"] = scan_z_send(1)
        if part == 2:
            scan_z_wait(1, marks["f1"])
            s = jnp.zeros((8, 128), F32)
            for k in range(NZ):
                zo[1, k] = s
                s = zr[1, k] + az_ref[k] * s
            marks["f2"] = scan_z_back(1)
        if part == 3:
            scan_z_back_wait(1, marks["f2"])
            s = jnp.concatenate([zp[1, k] for k in range(NZ)], 0)
            for k in range(NX):
                bo_ref[1, k] = s.astype(BF)
                if k < NX - 1:
                    s = xr[1, k].astype(F32) + ret(k) * s
            marks["f3"] = scan_x_back(1)
        if part == 4:
            scan_x_back_wait(1, marks["f3"])
            for i in range(4):
                cols = pl.ds(i * 128, 128)
                s = br_ref[1, i]
                ss[0, :, cols] = s
                ss[1, :, cols] = (a_ref[0, i][0:1, :] * s.astype(F32) + est[0, i]).astype(BF)

    def finish_gx(sp):
        rows = pl.ds(sp * SPAN, SPAN)
        gx[rows, :] = (gxf[rows, :] + te_ref[rows, :] * mm(b_ref[rows, :], qs[sp])).astype(BF)

    def project(first_o, count):
        def one(k, carry):
            o = (first_o + k) % NZ
            zz = (z + o) % NZ
            cols = pl.ds(pl.multiple_of((zz % 2) * 256, 256), 256)
            xacc[...] += mm(inpb[zz // 2, :, cols], wbuf[o].reshape(256, 512))
            return carry

        lax.fori_loop(0, count, one, 0)

    def own_states():
        xb = xacc[...].astype(BF)
        x_ref[...] = xb
        ex_ref[...] = (te_ref[...] * xb.astype(F32)).astype(BF)
        for sp in range(2):
            rows = pl.ds(sp * SPAN, SPAN)
            bt = b_ref[rows, :].T
            for i in range(4):
                est[sp, i] = mm(bt, ex_ref[rows, pl.ds(i * 128, 128)])

    rS = recv_slots(4)

    def part_of(j, k):
        return mm_nt(gx[...], wbuf[(2 * j + k + NZ - z) % NZ].reshape(256, 512))

    def rs_sib(d):
        j = ((y + d) % NY) * 2 + (1 - c)
        for k in (0, 1):
            pbuf[j, :, half[k]] = part_of(j, k).astype(BF)
        copy(pbuf.at[j], sibr.at[(y + d) % NY], rS + d, sib)

    rF, rN = recv_slots(2), recv_slots(4)

    def rs_own(d):
        yy = (y + d) % NY
        j = yy * 2 + c
        arrived(sibr.at[yy], rS + d)
        for k in (0, 1):
            pbuf[j, :, half[k]] = (part_of(j, k) + sibr[yy, :, half[k]].astype(F32)).astype(BF)
        if d == 2:
            copy(pbuf.at[j, :, half[1]], yfar.at[:, half[1]], rF + 1, at_y(1))
            copy(pbuf.at[j, :, half[0]], yfar.at[:, half[0]], rF + 0, at_y(3))
        if d == 1:
            copy(pbuf.at[j, :, half[0]], ynear.at[0, :, half[0]], rN + 0, at_y(1))
        if d == 3:
            copy(pbuf.at[j, :, half[1]], ynear.at[1, :, half[1]], rN + 1, at_y(3))

    def rs_pass():
        j = ((y + 1) % NY) * 2 + c
        arrived(yfar.at[:, half[1]], rF + 1)
        pbuf[j, :, 256:512] = (pbuf[j, :, 256:512].astype(F32) + yfar[:, 256:512].astype(F32)).astype(BF)
        copy(pbuf.at[j, :, half[1]], ynear.at[0, :, half[1]], rN + 2, at_y(1))
        j = ((y + 3) % NY) * 2 + c
        arrived(yfar.at[:, half[0]], rF + 0)
        pbuf[j, :, 0:256] = (pbuf[j, :, 0:256].astype(F32) + yfar[:, 0:256].astype(F32)).astype(BF)
        copy(pbuf.at[j, :, half[0]], ynear.at[1, :, half[0]], rN + 3, at_y(3))

    def rs_end():
        arrived(ynear.at[0, :, half[0]], rN + 0)
        arrived(ynear.at[1, :, half[1]], rN + 1)
        arrived(ynear.at[0, :, half[1]], rN + 2)
        arrived(ynear.at[1, :, half[0]], rN + 3)
        gi_ref[...] = (
            pbuf[head].astype(F32) + ynear[0].astype(F32) + ynear[1].astype(F32)
        ).astype(BF)

    def unit2(sp):
        rows = pl.ds(sp * SPAN, SPAN)
        dmt[sp] = jnp.zeros((SPAN, SPAN), F32)
        dcol[sp] = jnp.zeros((SPAN, 128), F32)

        def one(i, carry):
            cols = pl.ds(pl.multiple_of(i * 128, 128), 128)
            g2, x2 = g_ref[rows, cols], x_ref[rows, cols]
            mt = mt_ref[sp]
            for k in (0, 1):
                h = 2 * i + k
                xm = jnp.where(low if k == 0 else jnp.logical_not(low), x2, jnp.zeros_like(x2))
                p = mm_nt(xm, g2) * lt_ref[sp * 8 + h]
                dmt[sp] += p
                wm = p * mt
                drow[sp, pl.ds(h, 1), :] = jnp.sum(wm, axis=0, keepdims=True)
                dcol[sp] += jnp.where(lane == h, jnp.sum(wm, axis=1, keepdims=True), 0.0)
            return carry

        lax.fori_loop(0, 4, one, 0)

    ind = (iota((8, 512), 1) // 64 == iota((8, 512), 0)).astype(BF)

    def head_sums(value):
        hi = value.astype(BF)
        lo = (value - hi.astype(F32)).astype(BF)
        return mm_nt(ind, hi) + mm_nt(ind, lo)

    def grad_b_part(sp):
        rows = pl.ds(sp * SPAN, SPAN)
        pr[0, rows, :] = (mm(dmt[sp].astype(BF), c_ref[rows, :]) + mm_nt(ex_ref[rows, :], qs[sp])).astype(BF)

    def grad_c_inner(sp):
        rows = pl.ds(sp * SPAN, SPAN)
        gc_ref[rows, :] = mm_tn(dmt[sp].astype(BF), b_ref[rows, :])

    def grad_c_part(sp):
        rows = pl.ds(sp * SPAN, SPAN)
        pr[1, rows, :] = (gc_ref[rows, :] + mm_nt(v_ref[rows, :], ss[sp])).astype(BF)

    def decay_part(sp):
        rows = pl.ds(sp * SPAN, SPAN)
        u = mm(c_ref[rows, :], ss[sp])
        arow = jnp.concatenate([a_ref[sp, i][0:1, :] for i in range(4)], 1)
        cross = jnp.sum(qs[sp].astype(F32) * ss[sp].astype(F32), axis=0, keepdims=True) * arow
        is_last = iota((SPAN, 512), 0) == SPAN - 1
        vv = v_ref[rows, :].astype(F32) * u + jnp.where(is_last, cross, 0.0)
        tt = te_ref[rows, :] * x_ref[rows, :].astype(F32) * mm(b_ref[rows, :], qs[sp])
        dr = head_sums(vv) + drow[sp] - dcol[sp].T[0:8, :]
        gld_ref[:, rows] = mm(dr, (ti >= tj).astype(F32), EXACT) + mm(head_sums(tt), (ti < tj).astype(F32), EXACT)

    def mine(k):
        return pl.ds(pl.multiple_of(k * 64, 64), 64)

    def ps_send(which):
        base = recv_slots(8)
        for d in range(1, 8):
            to = (head + d) % 8
            copy(pr.at[which, mine(to), :], prr.at[which, head], base + d, at_head(d))
        prr[which, head] = pr[which, mine(head), :]
        return base

    def ps_sum(which, base):
        for d in range(1, 8):
            arrived(prr.at[which, (head + 8 - d) % 8], base + d)
        total = prr[which, 0].astype(F32)
        for k in range(1, 8):
            total = total + prr[which, k].astype(F32)
        pfin[which] = total.astype(BF)
        base = recv_slots(8)
        for d in range(1, 8):
            copy(pfin.at[which], pfull.at[which, mine(head), :], base + d, at_head(d))
        pfull[which, mine(head), :] = pfin[which]
        return base

    def ps_end(which, base, out):
        for d in range(1, 8):
            arrived(pfull.at[which, mine((head + 8 - d) % 8), :], base + d)
        out[...] = pfull[which].astype(F32)

    stores = []

    def put(src, dst):
        d = pltpu.make_async_copy(src, dst, load_sem.at[6 + len(stores)])
        d.start()
        stores.append(d)

    w_begin()
    input_begin()
    for d in loads:
        d.wait()
    w_own.wait()
    x_send((0,))
    first(0)
    p_start()
    b_step(1)
    first(1)
    ret_x()
    bscan(0)
    b_step(2)
    x_send((1, 2))
    xacc[...] = jnp.zeros_like(xacc)
    p_step(1)
    unit1(0, 0)
    b_step(3)
    x_send((3,))
    x_pass((0,))
    p_step(2)
    unit1(0, 1)
    b_step(4)
    x_pass((1, 2))
    x_end((0,))
    ret_z()
    bscan(1)
    input_pass(0)
    x_pass((3,))
    p_step(3)
    unit1(0, 2)
    b_step(5)
    x_send((4, 5))
    x_end((1, 2))
    x_end((3,))
    q_start()
    p_step(4)
    unit1(0, 3)
    b_step(6)
    x_send((6,))
    x_pass((4, 5))
    q_step(4)
    bscan(2)
    input_pass(1)
    p_step(5)
    unit1(1, 0)
    b_step(7)
    x_send((7,))
    x_pass((6,))
    q_step(5)
    p_step(6)
    unit1(1, 1)
    b_step(8)
    x_send((8,))
    x_end((4, 5))
    x_pass((7,))
    q_step(6)
    bscan(3)
    input_pass(2)
    p_step(7)
    unit1(1, 2)
    x_end((6,))
    x_pass((8,))
    q_step(7)
    unit1(1, 3)
    input_pass(3)
    project(NZ - 6, 13)
    p_step(8)
    x_end((7,))
    x_end((8,))
    q_step(8)
    project(7, 3)
    own_states()
    fscan(0)
    bscan(4)
    finish_gx(0)
    finish_gx(1)
    rs_sib(2)
    rs_sib(1)
    rs_own(2)
    fscan(1)
    rs_sib(3)
    rs_own(1)
    rs_sib(0)
    rs_own(3)
    rs_own(0)
    unit2(0)
    fscan(2)
    unit2(1)
    grad_b_part(0)
    grad_b_part(1)
    pb = ps_send(0)
    grad_c_inner(0)
    grad_c_inner(1)
    rs_pass()
    fscan(3)
    pb = ps_sum(0, pb)
    fscan(4)
    grad_c_part(0)
    grad_c_part(1)
    pc = ps_send(1)
    decay_part(0)
    pc = ps_sum(1, pc)
    decay_part(1)
    put(gld_ref, gld_hbm)
    ps_end(0, pb, gb_ref)
    put(gb_ref, gb_hbm)
    rs_end()
    put(gi_ref, gi_hbm)
    ps_end(1, pc, gc_ref)
    put(gc_ref, gc_hbm)
    for d in stores:
        d.wait()
    for d in sent:
        d.wait_send()
    assert counts["s"] <= N_SEND and counts["r"] <= N_RECV, counts


def local(inputs, w_in, b_rows, c_rows, log_decay, skip_gain, grad_out):
    hbm = pl.BlockSpec(memory_space=pl.ANY)
    V = pltpu.VMEM
    return pl.pallas_call(
        kernel,
        out_shape=(
            jax.ShapeDtypeStruct((T, 512), BF),
            jax.ShapeDtypeStruct((T, 128), F32),
            jax.ShapeDtypeStruct((T, 128), F32),
            jax.ShapeDtypeStruct((8, T), F32),
        ),
        in_specs=[hbm] * 5 + [pl.BlockSpec(memory_space=pltpu.SMEM), hbm],
        out_specs=(hbm,) * 4,
        scratch_shapes=[
            V((T, 128), BF),
            V((T, 128), BF),
            V((8, T), F32),
            V((T, 512), BF),
            V((T, 512), BF),
            V((T, 128), F32),
            V((T, 128), F32),
            V((8, T), F32),
            V((NZ, NX, 64, 512), BF),
            V((8, T, 512), BF),
            V((8, T, 512), BF),
            V((4, T, 512), BF),
            V((T, 512), BF),
            V((2, T, 512), BF),
            V((16, SPAN, SPAN), F32),
            V((2, SPAN, SPAN), F32),
            V((T, 512), F32),
            V((T, 512), BF),
            V((T, 512), F32),
            V((T, 512), BF),
            V((T, 512), F32),
            V((T, 512), BF),
            V((T, 512), BF),
            V((2, 8, SPAN), F32),
            V((2, SPAN, 128), F32),
            V((2, 4, 8, 128), F32),
            V((5, 8, 128), F32),
            V((4, 8, 128), F32),
            V((16, 8, 128), F32),
            V((2, 4, 128, 128), F32),
            V((2, 4, 128, 128), F32),
            V((2, 128, 512), BF),
            V((2, 128, 512), BF),
            V((2, 4, 128, 128), BF),
            V((2, 4, 128, 128), BF),
            V((2, 16, 8, 128), F32),
            V((2, 16, 8, 128), F32),
            V((2, 16, 8, 128), F32),
            V((2, 16, 8, 128), F32),
            V((2, 4, 128, 128), BF),
            V((2, 4, 128, 128), BF),
            V((2, SPAN, SPAN), F32),
            V((2, 8, SPAN), F32),
            V((2, SPAN, 128), F32),
            V((2, T, 128), BF),
            V((2, 8, 64, 128), BF),
            V((2, 64, 128), BF),
            V((2, T, 128), BF),
            pltpu.SemaphoreType.DMA((N_SEND,)),
            pltpu.SemaphoreType.DMA((N_RECV,)),
            pltpu.SemaphoreType.DMA((10,)),
        ],
        compiler_params=pltpu.CompilerParams(
            collective_id=0, has_side_effects=True, vmem_limit_bytes=60 * 1024 * 1024
        ),
        cost_estimate=pl.CostEstimate(flops=8 * 10**9, bytes_accessed=4 * 10**6, transcendentals=2 * 10**6),
    )(inputs, w_in, b_rows, c_rows, log_decay, skip_gain, grad_out)


def solution(mesh):
    in_specs = (
        P("ctx", "head"),
        P("ctx", "head"),
        P("ctx", None),
        P("ctx", None),
        P("head", "ctx"),
        P("head"),
        P("ctx", "head"),
    )
    out_specs = (P("ctx", "head"), P("ctx", None), P("ctx", None), P("head", "ctx"))
    return jax.shard_map(local, mesh=mesh, in_specs=in_specs, out_specs=out_specs, check_vma=False)
```

```python
import jax
import jax.numpy as jnp
from jax import lax
from jax.experimental import pallas as pl
from jax.experimental.pallas import tpu as pltpu
from jax.sharding import PartitionSpec as P

MESH = pl.DeviceIdType.MESH
BF = jnp.bfloat16
F32 = jnp.float32
EXACT = lax.Precision.HIGHEST
NX, NY, NZ = 4, 4, 16
SPAN = 256
T = 512
NEG = -1e30
Q_FROM = 4
FAR_FIRST = sorted(range(1, NZ), key=lambda d: -min(d, NZ - d))


def mm(a, b, precision=None):
    return lax.dot_general(a, b, (((1,), (0,)), ((), ())), precision=precision, preferred_element_type=F32)


def mm_nt(a, b, precision=None):
    return lax.dot_general(a, b, (((1,), (1,)), ((), ())), precision=precision, preferred_element_type=F32)


def mm_tn(a, b):
    return lax.dot_general(a, b, (((0,), (0,)), ((), ())), preferred_element_type=F32)


def iota(shape, dim):
    return lax.broadcasted_iota(jnp.int32, shape, dim)


N_SEND = 48
N_RECV = 137


def kernel(
    inp_ref, w_ref, b_hbm, c_hbm, ld_hbm, sk_ref, g_hbm,
    gi_hbm, gb_hbm, gc_hbm, gld_hbm,
    b_ref, c_ref, ld_ref, g_ref, gi_ref, gb_ref, gc_ref, gld_ref,
    wbuf, inpb, pbuf, sibr, yfar, ynear, lt_ref, mt_ref, gxf, gx, te_ref, v_ref, xacc, x_ref, ex_ref,
    rr_ref, rc_ref, a_ref, adev, ax_ref, az_ref,
    gst, est, qs, ss, sx_ref, xr, tz, zr, zo, zp, bo_ref, br_ref,
    dmt, drow, dcol, pr, prr, pfin, pfull,
    send_sem, recv_sem, load_sem,
):
    ctx = lax.axis_index("ctx")
    head = lax.axis_index("head")
    z, x = ctx // NX, ctx % NX
    y, c = head // 2, head % 2

    def at_x(d):
        return (z * NX + (x + d) % NX, head)

    def at_z(d):
        return (((z + d) % NZ) * NX + x, head)

    def at_y(d):
        return (ctx, ((y + d) % NY) * 2 + c)

    sib = (ctx, y * 2 + (1 - c))

    def at_head(d):
        return (ctx, (head + d) % 8)

    counts = {"s": 0, "r": 0}
    sent = []

    def recv_slots(n):
        base = counts["r"]
        counts["r"] += n
        return base

    def copy(src, dst, slot, device):
        k = counts["s"]
        counts["s"] += 1
        if k >= N_SEND:
            sent[k - N_SEND].wait_send()
        d = pltpu.make_async_remote_copy(
            src_ref=src, dst_ref=dst, send_sem=send_sem.at[k % N_SEND], recv_sem=recv_sem.at[slot],
            device_id=device, device_id_type=MESH,
        )
        d.start()
        sent.append(d)

    def arrived(dst, slot):
        pltpu.make_async_remote_copy(
            src_ref=dst, dst_ref=dst, send_sem=send_sem.at[0], recv_sem=recv_sem.at[slot],
            device_id=sib, device_id_type=MESH,
        ).wait_recv()

    loads = []
    for src, dst in ((ld_hbm, ld_ref), (c_hbm, c_ref), (g_hbm, g_ref), (b_hbm, b_ref)):
        d = pltpu.make_async_copy(src, dst, load_sem.at[len(loads)])
        d.start()
        loads.append(d)

    barrier = pltpu.get_barrier_semaphore()
    peers = [at_x(d) for d in range(1, NX)] + [at_z(d) for d in range(1, NZ)] + [at_head(d) for d in range(1, 8)]
    for peer in peers:
        pl.semaphore_signal(barrier, inc=1, device_id=peer, device_id_type=MESH)
    pl.semaphore_wait(barrier, len(peers))

    every = slice(None)
    pairs = (pl.ds(0, 2), pl.ds(2, 2))
    P_ = [(two, every, pl.ds(0, 128)) for two in pairs]
    Q_ = [(two, every, pl.ds(128, 128)) for two in pairs]

    def b_cols(s):
        return pl.ds(128, 384) if s < Q_FROM else pl.ds(256, 256)

    bz = (recv_slots(7) - 1, recv_slots(8) - 1)
    pz = [(recv_slots(8) - 1, recv_slots(7) - 1) for _ in range(2)]
    qz = [(recv_slots(9 - Q_FROM) - Q_FROM, recv_slots(8 - Q_FROM) - Q_FROM) for _ in range(2)]
    p0 = recv_slots(1)
    w_own = pltpu.make_async_copy(w_ref, wbuf.at[0, x], load_sem.at[4])
    left, right, far = (x + 3) % NX, (x + 1) % NX, (x + 2) % NX
    rows1, rows2 = pl.ds(0, 32), pl.ds(32, 32)

    def w_begin():
        for d in (2, 1, 3):
            copy(w_ref.at[:, pl.ds(0, 128)], wbuf.at[0, x, :, pl.ds(0, 128)], p0, at_x(d))
        copy(w_ref.at[:, b_cols(1)], wbuf.at[15, x, :, b_cols(1)], bz[0] + 1, at_z(1))
        copy(w_ref.at[:, b_cols(1)], wbuf.at[1, x, :, b_cols(1)], bz[1] + 1, at_z(NZ - 1))
        w_own.start()

    def z_send(s, region, slots, to_right, to_left):
        if to_right:
            copy(wbuf.at[((17 - s) % NZ,) + region], wbuf.at[(16 - s,) + region], slots[0] + s, at_z(1))
        if to_left:
            copy(wbuf.at[(s - 1,) + region], wbuf.at[(s,) + region], slots[1] + s, at_z(NZ - 1))

    def p_start():
        arrived(wbuf.at[0, pl.ds(0, 3), every, pl.ds(0, 128)], p0)
        for k in (0, 1):
            z_send(1, P_[k], pz[k], True, True)

    def p_step(s):
        for k in (0, 1):
            a_step(s, P_[k], pz[k])

    def q_start():
        for k in (0, 1):
            z_send(Q_FROM, Q_[k], qz[k], True, True)

    def q_step(s):
        for k in (0, 1):
            a_step(s, Q_[k], qz[k])

    def a_step(s, region, slots):
        arrived(wbuf.at[(16 - s,) + region], slots[0] + s)
        if s < 8:
            z_send(s + 1, region, slots, True, False)
            arrived(wbuf.at[(s,) + region], slots[1] + s)
            z_send(s + 1, region, slots, False, s < 7)

    def b_step(s):
        if s < 8:
            arrived(wbuf.at[16 - s, x, :, b_cols(s)], bz[0] + s)
            z_send(s + 1, (x, every, b_cols(s + 1)), bz, s < 7, False)
        arrived(wbuf.at[s, x, :, b_cols(s)], bz[1] + s)
        z_send(s + 1, (x, every, b_cols(s + 1)), bz, False, s < 8)

    slots_x = {}

    def b_spans(batch):
        lo, hi = batch[0], batch[-1]
        n = hi - lo + 1
        if lo == 0 or lo == 8:
            return [(pl.ds(lo, 1), batch)]
        return [(pl.ds(16 - hi, n), batch), (pl.ds(lo, n), batch)]

    def x_send(batch):
        cols = b_cols(batch[0])
        for k, (o, _) in enumerate(b_spans(batch)):
            base = slots_x[batch, k] = recv_slots(3)
            blk = wbuf.at[o, x, :, cols]
            copy(blk, blk, base + 0, at_x(1))
            copy(blk, blk, base + 1, at_x(3))

    def x_pass(batch):
        cols = b_cols(batch[0])
        for k, (o, _) in enumerate(b_spans(batch)):
            base = slots_x[batch, k]
            arrived(wbuf.at[o, left, :, cols], base + 0)
            blk = wbuf.at[o, left, rows1, cols]
            copy(blk, blk, base + 2, at_x(1))
            arrived(wbuf.at[o, right, :, cols], base + 1)
            blk = wbuf.at[o, right, rows2, cols]
            copy(blk, blk, base + 2, at_x(3))

    def x_end(batch):
        cols = b_cols(batch[0])
        for k, (o, _) in enumerate(b_spans(batch)):
            base = slots_x[batch, k]
            arrived(wbuf.at[o, far, :, cols], base + 2)

    half = (pl.ds(0, 256), pl.ds(256, 256))
    iR, iL, iF, iS = recv_slots(2), recv_slots(2), recv_slots(2), recv_slots(7)

    def ihead(d):
        return ((y + d) % NY) * 2 + c

    i_own = pltpu.make_async_copy(inp_ref, inpb.at[head], load_sem.at[5])

    def input_begin():
        i_own.start()
        copy(inp_ref.at[:, half[0]], inpb.at[head, :, half[0]], iR + 0, at_y(1))
        copy(inp_ref.at[:, half[1]], inpb.at[head, :, half[1]], iL + 1, at_y(3))
        copy(inp_ref.at[:, half[1]], inpb.at[head, :, half[1]], iR + 1, at_y(1))
        copy(inp_ref.at[:, half[0]], inpb.at[head, :, half[0]], iL + 0, at_y(3))
        copy(inp_ref, inpb.at[head], iS + 0, sib)

    def input_pass(part):
        left, right, far = ihead(3), ihead(1), ihead(2)
        if part == 0:
            arrived(inpb.at[left, :, half[0]], iR + 0)
            copy(inpb.at[left, :, half[0]], inpb.at[left, :, half[0]], iF + 0, at_y(1))
            arrived(inpb.at[right, :, half[1]], iL + 1)
            copy(inpb.at[right, :, half[1]], inpb.at[right, :, half[1]], iF + 1, at_y(3))
            copy(inpb.at[left, :, half[0]], inpb.at[left, :, half[0]], iS + 1, sib)
            copy(inpb.at[right, :, half[1]], inpb.at[right, :, half[1]], iS + 2, sib)
        if part == 1:
            arrived(inpb.at[left, :, half[1]], iR + 1)
            copy(inpb.at[left, :, half[1]], inpb.at[left, :, half[1]], iS + 3, sib)
            arrived(inpb.at[right, :, half[0]], iL + 0)
            copy(inpb.at[right, :, half[0]], inpb.at[right, :, half[0]], iS + 4, sib)
        if part == 2:
            for k in (0, 1):
                arrived(inpb.at[far, :, half[k]], iF + k)
                copy(inpb.at[far, :, half[k]], inpb.at[far, :, half[k]], iS + 5 + k, sib)
        if part == 3:
            i_own.wait()

            def other(d):
                return ((y + d) % NY) * 2 + (1 - c)
            arrived(inpb.at[other(0)], iS + 0)
            arrived(inpb.at[other(3), :, half[0]], iS + 1)
            arrived(inpb.at[other(1), :, half[1]], iS + 2)
            arrived(inpb.at[other(3), :, half[1]], iS + 3)
            arrived(inpb.at[other(1), :, half[0]], iS + 4)
            for k in (0, 1):
                arrived(inpb.at[other(2), :, half[k]], iS + 5 + k)

    lane = iota((SPAN, 128), 1)
    low = lane < 64
    lowrow = iota((1, 128), 1) < 64
    ti, tj = iota((SPAN, SPAN), 0), iota((SPAN, SPAN), 1)
    upto = ti <= tj

    def pair(col, i):
        return jnp.where(low, col[:, 2 * i:2 * i + 1], col[:, 2 * i + 1:2 * i + 2])

    def pair_row(row, i):
        return jnp.where(lowrow, row[:, 2 * i:2 * i + 1], row[:, 2 * i + 1:2 * i + 2])

    def first(sp):
        rows = pl.ds(sp * SPAN, SPAN)
        rr = mm(ld_ref[:, rows], upto.astype(F32), EXACT)
        rc = jnp.concatenate([rr, jnp.zeros((120, SPAN), F32)], 0).T
        rr_ref[sp] = rr
        rc_ref[sp] = rc
        last = rc[SPAN - 1:SPAN, :]
        ec, tc, al = jnp.exp(rc), jnp.exp(last - rc), jnp.exp(last)
        ct = c_ref[rows, :].T
        for i in range(4):
            cols = pl.ds(i * 128, 128)
            v = (g_ref[rows, cols].astype(F32) * pair(ec, i)).astype(BF)
            v_ref[rows, cols] = v
            te_ref[rows, cols] = pair(tc, i)
            a_ref[sp, i] = jnp.broadcast_to(pair_row(al, i), (8, 128))
            gst[sp, i] = mm(ct, v)
        mt_ref[sp] = mm_nt(b_ref[rows, :], c_ref[rows, :])

    def unit1(sp, i):
        rows, cols = pl.ds(sp * SPAN, SPAN), pl.ds(i * 128, 128)
        g2 = g_ref[rows, cols]
        mt = mt_ref[sp]
        parts = []
        for k in (0, 1):
            h = 2 * i + k
            diff = rr_ref[sp, h:h + 1, :] - rc_ref[sp, :, h:h + 1]
            lt = jnp.exp(jnp.where(upto, diff, NEG))
            lt_ref[sp * 8 + h] = lt
            parts.append(mm((lt * mt).astype(BF), g2))
        skip = jnp.where(lowrow, sk_ref[2 * i], sk_ref[2 * i + 1])
        gxf[rows, cols] = jnp.where(low, parts[0], parts[1]) + skip * g2.astype(F32)

    def scan_x_send(which, state):
        base = recv_slots(1)
        for i in range(4):
            sx_ref[which, i] = state(i).astype(BF)
        for d in (1, 3, 2):
            to = (x + d) % NX
            copy(sx_ref.at[which, to], xr.at[which, x], base, at_x(d))
        xr[which, x] = sx_ref[which, x]
        return base

    def scan_x_wait(which, base):
        arrived(xr.at[which, pl.ds(0, NX - 1)], base)

    def scan_z_send(which):
        base = recv_slots(1)
        for d in FAR_FIRST:
            to = (z + d) % NZ
            copy(tz.at[which, to], zr.at[which, z], base, at_z(d))
        zr[which, z] = tz[which, z]
        return base

    def scan_z_wait(which, base):
        arrived(zr.at[which, pl.ds(0, NZ - 1)], base)

    def scan_z_back(which):
        base = recv_slots(1)
        for d in FAR_FIRST:
            to = (z + d) % NZ
            copy(zo.at[which, to], zp.at[which, z], base, at_z(d))
        zp[which, z] = zo[which, z]
        return base

    def scan_z_back_wait(which, base):
        arrived(zp.at[which, pl.ds(0, NZ - 1)], base)

    def scan_x_back(which):
        base = recv_slots(1)
        for d in (1, 3, 2):
            to = (x + d) % NX
            copy(bo_ref.at[which, to], br_ref.at[which, x], base, at_x(d))
        br_ref[which, x] = bo_ref[which, x]
        return base

    def scan_x_back_wait(which, base):
        arrived(br_ref.at[which, pl.ds(0, NX - 1)], base)

    marks = {}

    def ret_x():
        base = recv_slots(1)
        for i in range(4):
            adev[i] = a_ref[0, i] * a_ref[1, i]
        for d in (1, 3, 2):
            to = (x + d) % NX
            copy(adev.at[to], ax_ref.at[x], base, at_x(d))
        ax_ref[x] = adev[x]
        marks["ax"] = base

    def ret_z():
        arrived(ax_ref.at[pl.ds(0, NX - 1)], marks["ax"])
        base = recv_slots(1)
        adev[4] = ax_ref[0] * ax_ref[1] * ax_ref[2] * ax_ref[3]
        for d in FAR_FIRST:
            copy(adev.at[4], az_ref.at[z], base, at_z(d))
        az_ref[z] = adev[4]
        marks["az"] = base

    def ret_wait():
        arrived(az_ref.at[pl.ds(0, NZ - 1)], marks["az"])

    def ret(k):
        return ax_ref[k][0:1, :]

    def put_total(which, total):
        for k in range(NZ):
            tz[which, k] = total[8 * k:8 * k + 8, :]

    def bscan(part):
        if part == 0:
            marks["b0"] = scan_x_send(0, lambda i: gst[0, i] + a_ref[0, i][0:1, :] * gst[1, i])
        if part == 1:
            scan_x_wait(0, marks["b0"])
            total = xr[0, 3].astype(F32)
            for k in (2, 1, 0):
                total = xr[0, k].astype(F32) + ret(k) * total
            put_total(0, total)
            marks["b1"] = scan_z_send(0)
        if part == 2:
            ret_wait()
            scan_z_wait(0, marks["b1"])
            q = jnp.zeros((8, 128), F32)
            for k in range(NZ - 1, -1, -1):
                zo[0, k] = q
                q = zr[0, k] + az_ref[k] * q
            marks["b2"] = scan_z_back(0)
        if part == 3:
            scan_z_back_wait(0, marks["b2"])
            q = jnp.concatenate([zp[0, k] for k in range(NZ)], 0)
            for k in (3, 2, 1, 0):
                bo_ref[0, k] = q.astype(BF)
                if k:
                    q = xr[0, k].astype(F32) + ret(k) * q
            marks["b3"] = scan_x_back(0)
        if part == 4:
            scan_x_back_wait(0, marks["b3"])
            for i in range(4):
                cols = pl.ds(i * 128, 128)
                q = br_ref[0, i]
                qs[1, :, cols] = q
                qs[0, :, cols] = (gst[1, i] + a_ref[1, i][0:1, :] * q.astype(F32)).astype(BF)

    def fscan(part):
        if part == 0:
            marks["f0"] = scan_x_send(1, lambda i: a_ref[1, i][0:1, :] * est[0, i] + est[1, i])
        if part == 1:
            scan_x_wait(1, marks["f0"])
            total = xr[1, 0].astype(F32)
            for k in (1, 2, 3):
                total = xr[1, k].astype(F32) + ret(k) * total
            put_total(1, total)
            marks["f1"] = scan_z_send(1)
        if part == 2:
            scan_z_wait(1, marks["f1"])
            s = jnp.zeros((8, 128), F32)
            for k in range(NZ):
                zo[1, k] = s
                s = zr[1, k] + az_ref[k] * s
            marks["f2"] = scan_z_back(1)
        if part == 3:
            scan_z_back_wait(1, marks["f2"])
            s = jnp.concatenate([zp[1, k] for k in range(NZ)], 0)
            for k in range(NX):
                bo_ref[1, k] = s.astype(BF)
                if k < NX - 1:
                    s = xr[1, k].astype(F32) + ret(k) * s
            marks["f3"] = scan_x_back(1)
        if part == 4:
            scan_x_back_wait(1, marks["f3"])
            for i in range(4):
                cols = pl.ds(i * 128, 128)
                s = br_ref[1, i]
                ss[0, :, cols] = s
                ss[1, :, cols] = (a_ref[0, i][0:1, :] * s.astype(F32) + est[0, i]).astype(BF)

    def finish_gx(sp):
        rows = pl.ds(sp * SPAN, SPAN)
        gx[rows, :] = (gxf[rows, :] + te_ref[rows, :] * mm(b_ref[rows, :], qs[sp])).astype(BF)

    def project(first_o, count):
        def one(k, carry):
            o = (first_o + k) % NZ
            zz = (z + o) % NZ
            cols = pl.ds(pl.multiple_of((zz % 2) * 256, 256), 256)
            xacc[...] += mm(inpb[zz // 2, :, cols], wbuf[o].reshape(256, 512))
            return carry

        lax.fori_loop(0, count, one, 0)

    def own_states():
        xb = xacc[...].astype(BF)
        x_ref[...] = xb
        ex_ref[...] = (te_ref[...] * xb.astype(F32)).astype(BF)
        for sp in range(2):
            rows = pl.ds(sp * SPAN, SPAN)
            bt = b_ref[rows, :].T
            for i in range(4):
                est[sp, i] = mm(bt, ex_ref[rows, pl.ds(i * 128, 128)])

    rS = recv_slots(4)

    def part_of(j, k):
        return mm_nt(gx[...], wbuf[(2 * j + k + NZ - z) % NZ].reshape(256, 512))

    def rs_sib(d):
        j = ((y + d) % NY) * 2 + (1 - c)
        for k in (0, 1):
            pbuf[j, :, half[k]] = part_of(j, k).astype(BF)
        copy(pbuf.at[j], sibr.at[(y + d) % NY], rS + d, sib)

    rF, rN = recv_slots(2), recv_slots(4)

    def rs_own(d):
        yy = (y + d) % NY
        j = yy * 2 + c
        arrived(sibr.at[yy], rS + d)
        for k in (0, 1):
            pbuf[j, :, half[k]] = (part_of(j, k) + sibr[yy, :, half[k]].astype(F32)).astype(BF)
        if d == 2:
            copy(pbuf.at[j, :, half[1]], yfar.at[:, half[1]], rF + 1, at_y(1))
            copy(pbuf.at[j, :, half[0]], yfar.at[:, half[0]], rF + 0, at_y(3))
        if d == 1:
            copy(pbuf.at[j, :, half[0]], ynear.at[0, :, half[0]], rN + 0, at_y(1))
        if d == 3:
            copy(pbuf.at[j, :, half[1]], ynear.at[1, :, half[1]], rN + 1, at_y(3))

    def rs_pass():
        j = ((y + 1) % NY) * 2 + c
        arrived(yfar.at[:, half[1]], rF + 1)
        pbuf[j, :, 256:512] = (pbuf[j, :, 256:512].astype(F32) + yfar[:, 256:512].astype(F32)).astype(BF)
        copy(pbuf.at[j, :, half[1]], ynear.at[0, :, half[1]], rN + 2, at_y(1))
        j = ((y + 3) % NY) * 2 + c
        arrived(yfar.at[:, half[0]], rF + 0)
        pbuf[j, :, 0:256] = (pbuf[j, :, 0:256].astype(F32) + yfar[:, 0:256].astype(F32)).astype(BF)
        copy(pbuf.at[j, :, half[0]], ynear.at[1, :, half[0]], rN + 3, at_y(3))

    def rs_end():
        arrived(ynear.at[0, :, half[0]], rN + 0)
        arrived(ynear.at[1, :, half[1]], rN + 1)
        arrived(ynear.at[0, :, half[1]], rN + 2)
        arrived(ynear.at[1, :, half[0]], rN + 3)
        gi_ref[...] = (
            pbuf[head].astype(F32) + ynear[0].astype(F32) + ynear[1].astype(F32)
        ).astype(BF)

    def unit2(sp):
        rows = pl.ds(sp * SPAN, SPAN)
        dmt[sp] = jnp.zeros((SPAN, SPAN), F32)
        dcol[sp] = jnp.zeros((SPAN, 128), F32)

        def one(i, carry):
            cols = pl.ds(pl.multiple_of(i * 128, 128), 128)
            g2, x2 = g_ref[rows, cols], x_ref[rows, cols]
            mt = mt_ref[sp]
            for k in (0, 1):
                h = 2 * i + k
                xm = jnp.where(low if k == 0 else jnp.logical_not(low), x2, jnp.zeros_like(x2))
                p = mm_nt(xm, g2) * lt_ref[sp * 8 + h]
                dmt[sp] += p
                wm = p * mt
                drow[sp, pl.ds(h, 1), :] = jnp.sum(wm, axis=0, keepdims=True)
                dcol[sp] += jnp.where(lane == h, jnp.sum(wm, axis=1, keepdims=True), 0.0)
            return carry

        lax.fori_loop(0, 4, one, 0)

    ind = (iota((8, 512), 1) // 64 == iota((8, 512), 0)).astype(BF)

    def head_sums(value):
        hi = value.astype(BF)
        lo = (value - hi.astype(F32)).astype(BF)
        return mm_nt(ind, hi) + mm_nt(ind, lo)

    def grad_b_part(sp):
        rows = pl.ds(sp * SPAN, SPAN)
        pr[0, rows, :] = (mm(dmt[sp].astype(BF), c_ref[rows, :]) + mm_nt(ex_ref[rows, :], qs[sp])).astype(BF)

    def grad_c_inner(sp):
        rows = pl.ds(sp * SPAN, SPAN)
        gc_ref[rows, :] = mm_tn(dmt[sp].astype(BF), b_ref[rows, :])

    def grad_c_part(sp):
        rows = pl.ds(sp * SPAN, SPAN)
        pr[1, rows, :] = (gc_ref[rows, :] + mm_nt(v_ref[rows, :], ss[sp])).astype(BF)

    def decay_part(sp):
        rows = pl.ds(sp * SPAN, SPAN)
        u = mm(c_ref[rows, :], ss[sp])
        arow = jnp.concatenate([a_ref[sp, i][0:1, :] for i in range(4)], 1)
        cross = jnp.sum(qs[sp].astype(F32) * ss[sp].astype(F32), axis=0, keepdims=True) * arow
        is_last = iota((SPAN, 512), 0) == SPAN - 1
        vv = v_ref[rows, :].astype(F32) * u + jnp.where(is_last, cross, 0.0)
        tt = te_ref[rows, :] * x_ref[rows, :].astype(F32) * mm(b_ref[rows, :], qs[sp])
        dr = head_sums(vv) + drow[sp] - dcol[sp].T[0:8, :]
        gld_ref[:, rows] = mm(dr, (ti >= tj).astype(F32), EXACT) + mm(head_sums(tt), (ti < tj).astype(F32), EXACT)

    def mine(k):
        return pl.ds(pl.multiple_of(k * 64, 64), 64)

    def ps_send(which):
        base = recv_slots(1)
        for d in (4, 3, 5, 2, 6, 1, 7):
            to = (head + d) % 8
            copy(pr.at[which, mine(to), :], prr.at[which, head], base, at_head(d))
        prr[which, head] = pr[which, mine(head), :]
        return base

    def ps_sum(which, base):
        arrived(prr.at[which, pl.ds(0, 7)], base)
        total = prr[which, 0].astype(F32)
        for k in range(1, 8):
            total = total + prr[which, k].astype(F32)
        pfin[which] = total.astype(BF)
        base = recv_slots(1)
        for d in (4, 3, 5, 2, 6, 1, 7):
            copy(pfin.at[which], pfull.at[which, mine(head), :], base, at_head(d))
        pfull[which, mine(head), :] = pfin[which]
        return base

    def ps_end(which, base, out):
        arrived(pfull.at[which, pl.ds(0, 448), :], base)
        out[...] = pfull[which].astype(F32)

    stores = []

    def put(src, dst):
        d = pltpu.make_async_copy(src, dst, load_sem.at[6 + len(stores)])
        d.start()
        stores.append(d)

    w_begin()
    input_begin()
    for d in loads:
        d.wait()
    w_own.wait()
    x_send((0,))
    first(0)
    p_start()
    b_step(1)
    first(1)
    ret_x()
    bscan(0)
    b_step(2)
    x_send((1, 2))
    xacc[...] = jnp.zeros_like(xacc)
    p_step(1)
    unit1(0, 0)
    b_step(3)
    x_send((3,))
    x_pass((0,))
    p_step(2)
    unit1(0, 1)
    b_step(4)
    x_pass((1, 2))
    x_end((0,))
    ret_z()
    bscan(1)
    input_pass(0)
    x_pass((3,))
    p_step(3)
    unit1(0, 2)
    b_step(5)
    x_send((4, 5))
    x_end((1, 2))
    x_end((3,))
    q_start()
    p_step(4)
    unit1(0, 3)
    b_step(6)
    x_send((6,))
    x_pass((4, 5))
    q_step(4)
    bscan(2)
    input_pass(1)
    p_step(5)
    unit1(1, 0)
    b_step(7)
    x_send((7,))
    x_pass((6,))
    q_step(5)
    p_step(6)
    unit1(1, 1)
    b_step(8)
    x_send((8,))
    x_end((4, 5))
    x_pass((7,))
    q_step(6)
    bscan(3)
    input_pass(2)
    p_step(7)
    unit1(1, 2)
    x_end((6,))
    x_pass((8,))
    q_step(7)
    unit1(1, 3)
    input_pass(3)
    project(NZ - 6, 13)
    p_step(8)
    x_end((7,))
    x_end((8,))
    q_step(8)
    project(7, 3)
    own_states()
    fscan(0)
    bscan(4)
    finish_gx(0)
    finish_gx(1)
    rs_sib(2)
    rs_sib(1)
    rs_own(2)
    fscan(1)
    rs_sib(3)
    rs_own(1)
    rs_sib(0)
    rs_own(3)
    rs_own(0)
    unit2(0)
    fscan(2)
    unit2(1)
    grad_b_part(0)
    grad_b_part(1)
    pb = ps_send(0)
    grad_c_inner(0)
    grad_c_inner(1)
    rs_pass()
    fscan(3)
    pb = ps_sum(0, pb)
    fscan(4)
    grad_c_part(0)
    grad_c_part(1)
    pc = ps_send(1)
    decay_part(0)
    pc = ps_sum(1, pc)
    decay_part(1)
    put(gld_ref, gld_hbm)
    ps_end(0, pb, gb_ref)
    put(gb_ref, gb_hbm)
    rs_end()
    put(gi_ref, gi_hbm)
    ps_end(1, pc, gc_ref)
    put(gc_ref, gc_hbm)
    for d in stores:
        d.wait()
    for d in sent[-N_SEND:]:
        d.wait_send()
    assert counts["r"] == N_RECV, counts


def local(inputs, w_in, b_rows, c_rows, log_decay, skip_gain, grad_out):
    hbm = pl.BlockSpec(memory_space=pl.ANY)
    V = pltpu.VMEM
    return pl.pallas_call(
        kernel,
        out_shape=(
            jax.ShapeDtypeStruct((T, 512), BF),
            jax.ShapeDtypeStruct((T, 128), F32),
            jax.ShapeDtypeStruct((T, 128), F32),
            jax.ShapeDtypeStruct((8, T), F32),
        ),
        in_specs=[hbm] * 5 + [pl.BlockSpec(memory_space=pltpu.SMEM), hbm],
        out_specs=(hbm,) * 4,
        scratch_shapes=[
            V((T, 128), BF),
            V((T, 128), BF),
            V((8, T), F32),
            V((T, 512), BF),
            V((T, 512), BF),
            V((T, 128), F32),
            V((T, 128), F32),
            V((8, T), F32),
            V((NZ, NX, 64, 512), BF),
            V((8, T, 512), BF),
            V((8, T, 512), BF),
            V((4, T, 512), BF),
            V((T, 512), BF),
            V((2, T, 512), BF),
            V((16, SPAN, SPAN), F32),
            V((2, SPAN, SPAN), F32),
            V((T, 512), F32),
            V((T, 512), BF),
            V((T, 512), F32),
            V((T, 512), BF),
            V((T, 512), F32),
            V((T, 512), BF),
            V((T, 512), BF),
            V((2, 8, SPAN), F32),
            V((2, SPAN, 128), F32),
            V((2, 4, 8, 128), F32),
            V((5, 8, 128), F32),
            V((4, 8, 128), F32),
            V((16, 8, 128), F32),
            V((2, 4, 128, 128), F32),
            V((2, 4, 128, 128), F32),
            V((2, 128, 512), BF),
            V((2, 128, 512), BF),
            V((2, 4, 128, 128), BF),
            V((2, 4, 128, 128), BF),
            V((2, 16, 8, 128), F32),
            V((2, 16, 8, 128), F32),
            V((2, 16, 8, 128), F32),
            V((2, 16, 8, 128), F32),
            V((2, 4, 128, 128), BF),
            V((2, 4, 128, 128), BF),
            V((2, SPAN, SPAN), F32),
            V((2, 8, SPAN), F32),
            V((2, SPAN, 128), F32),
            V((2, T, 128), BF),
            V((2, 8, 64, 128), BF),
            V((2, 64, 128), BF),
            V((2, T, 128), BF),
            pltpu.SemaphoreType.DMA((N_SEND,)),
            pltpu.SemaphoreType.DMA((N_RECV,)),
            pltpu.SemaphoreType.DMA((10,)),
        ],
        compiler_params=pltpu.CompilerParams(
            collective_id=0, has_side_effects=True, vmem_limit_bytes=60 * 1024 * 1024
        ),
        cost_estimate=pl.CostEstimate(flops=8 * 10**9, bytes_accessed=4 * 10**6, transcendentals=2 * 10**6),
    )(inputs, w_in, b_rows, c_rows, log_decay, skip_gain, grad_out)


def solution(mesh):
    in_specs = (
        P("ctx", "head"),
        P("ctx", "head"),
        P("ctx", None),
        P("ctx", None),
        P("head", "ctx"),
        P("head"),
        P("ctx", "head"),
    )
    out_specs = (P("ctx", "head"), P("ctx", None), P("ctx", None), P("head", "ctx"))
    return jax.shard_map(local, mesh=mesh, in_specs=in_specs, out_specs=out_specs, check_vma=False)
```

```python
import jax
import jax.numpy as jnp
from jax import lax
from jax.experimental import pallas as pl
from jax.experimental.pallas import tpu as pltpu
from jax.sharding import PartitionSpec as P

MESH = pl.DeviceIdType.MESH
BF = jnp.bfloat16
F32 = jnp.float32
EXACT = lax.Precision.HIGHEST
NX, NY, NZ = 4, 4, 16
SPAN = 256
T = 512
NEG = -1e30
Q_FROM = 4
FAR_FIRST = sorted(range(1, NZ), key=lambda d: -min(d, NZ - d))


def mm(a, b, precision=None):
    return lax.dot_general(a, b, (((1,), (0,)), ((), ())), precision=precision, preferred_element_type=F32)


def mm_nt(a, b, precision=None):
    return lax.dot_general(a, b, (((1,), (1,)), ((), ())), precision=precision, preferred_element_type=F32)


def mm_tn(a, b):
    return lax.dot_general(a, b, (((0,), (0,)), ((), ())), preferred_element_type=F32)


def iota(shape, dim):
    return lax.broadcasted_iota(jnp.int32, shape, dim)


N_SEND = 32
N_RECV = 137


def kernel(
    inp_ref, w_ref, b_hbm, c_hbm, ld_hbm, sk_ref, g_hbm,
    gi_hbm, gb_hbm, gc_hbm, gld_hbm,
    b_ref, c_ref, ld_ref, g_ref, gi_ref, gb_ref, gc_ref, gld_ref,
    wbuf, inpb, pbuf, sibr, yfar, ynear, lt_ref, mt_ref, gxf, gx, te_ref, v_ref, xacc, x_ref, ex_ref,
    rr_ref, rc_ref, a_ref, adev, ax_ref, az_ref,
    gst, est, qs, ss, sx_ref, xr, tz, zr, zo, zp, bo_ref, br_ref,
    dmt, drow, dcol, pr, prr, pfin, pfull,
    send_sem, recv_sem, load_sem,
):
    ctx = lax.axis_index("ctx")
    head = lax.axis_index("head")
    z, x = ctx // NX, ctx % NX
    y, c = head // 2, head % 2

    def at_x(d):
        return (z * NX + (x + d) % NX, head)

    def at_z(d):
        return (((z + d) % NZ) * NX + x, head)

    def at_y(d):
        return (ctx, ((y + d) % NY) * 2 + c)

    sib = (ctx, y * 2 + (1 - c))

    def at_head(d):
        return (ctx, (head + d) % 8)

    counts = {"s": 0, "r": 0}
    sent = []

    def recv_slots(n):
        base = counts["r"]
        counts["r"] += n
        return base

    def copy(src, dst, slot, device):
        k = counts["s"]
        counts["s"] += 1
        if k >= N_SEND:
            sent[k - N_SEND].wait_send()
        d = pltpu.make_async_remote_copy(
            src_ref=src, dst_ref=dst, send_sem=send_sem.at[k % N_SEND], recv_sem=recv_sem.at[slot],
            device_id=device, device_id_type=MESH,
        )
        d.start()
        sent.append(d)

    def arrived(dst, slot):
        pltpu.make_async_remote_copy(
            src_ref=dst, dst_ref=dst, send_sem=send_sem.at[0], recv_sem=recv_sem.at[slot],
            device_id=sib, device_id_type=MESH,
        ).wait_recv()

    loads = []
    for src, dst in ((ld_hbm, ld_ref), (c_hbm, c_ref), (g_hbm, g_ref), (b_hbm, b_ref)):
        d = pltpu.make_async_copy(src, dst, load_sem.at[len(loads)])
        d.start()
        loads.append(d)

    barrier = pltpu.get_barrier_semaphore()
    peers = [at_x(d) for d in range(1, NX)] + [at_z(d) for d in range(1, NZ)] + [at_head(d) for d in range(1, 8)]
    for peer in peers:
        pl.semaphore_signal(barrier, inc=1, device_id=peer, device_id_type=MESH)
    pl.semaphore_wait(barrier, len(peers))

    every = slice(None)
    pairs = (pl.ds(0, 2), pl.ds(2, 2))
    P_ = [(two, every, pl.ds(0, 128)) for two in pairs]
    Q_ = [(two, every, pl.ds(128, 128)) for two in pairs]

    def b_cols(s):
        return pl.ds(128, 384) if s < Q_FROM else pl.ds(256, 256)

    bz = (recv_slots(7) - 1, recv_slots(8) - 1)
    pz = [(recv_slots(8) - 1, recv_slots(7) - 1) for _ in range(2)]
    qz = [(recv_slots(9 - Q_FROM) - Q_FROM, recv_slots(8 - Q_FROM) - Q_FROM) for _ in range(2)]
    p0 = recv_slots(1)
    w_own = pltpu.make_async_copy(w_ref, wbuf.at[0, x], load_sem.at[4])
    left, right, far = (x + 3) % NX, (x + 1) % NX, (x + 2) % NX
    rows1, rows2 = pl.ds(0, 32), pl.ds(32, 32)

    def w_begin():
        for d in (2, 1, 3):
            copy(w_ref.at[:, pl.ds(0, 128)], wbuf.at[0, x, :, pl.ds(0, 128)], p0, at_x(d))
        copy(w_ref.at[:, b_cols(1)], wbuf.at[15, x, :, b_cols(1)], bz[0] + 1, at_z(1))
        copy(w_ref.at[:, b_cols(1)], wbuf.at[1, x, :, b_cols(1)], bz[1] + 1, at_z(NZ - 1))
        w_own.start()

    def z_send(s, region, slots, to_right, to_left):
        if to_right:
            copy(wbuf.at[((17 - s) % NZ,) + region], wbuf.at[(16 - s,) + region], slots[0] + s, at_z(1))
        if to_left:
            copy(wbuf.at[(s - 1,) + region], wbuf.at[(s,) + region], slots[1] + s, at_z(NZ - 1))

    def p_start():
        arrived(wbuf.at[0, pl.ds(0, 3), every, pl.ds(0, 128)], p0)
        for k in (0, 1):
            z_send(1, P_[k], pz[k], True, True)

    def p_step(s):
        for k in (0, 1):
            a_step(s, P_[k], pz[k])

    def q_start():
        for k in (0, 1):
            z_send(Q_FROM, Q_[k], qz[k], True, True)

    def q_step(s):
        for k in (0, 1):
            a_step(s, Q_[k], qz[k])

    def a_step(s, region, slots):
        arrived(wbuf.at[(16 - s,) + region], slots[0] + s)
        if s < 8:
            z_send(s + 1, region, slots, True, False)
            arrived(wbuf.at[(s,) + region], slots[1] + s)
            z_send(s + 1, region, slots, False, s < 7)

    def b_step(s):
        if s < 8:
            arrived(wbuf.at[16 - s, x, :, b_cols(s)], bz[0] + s)
            z_send(s + 1, (x, every, b_cols(s + 1)), bz, s < 7, False)
        arrived(wbuf.at[s, x, :, b_cols(s)], bz[1] + s)
        z_send(s + 1, (x, every, b_cols(s + 1)), bz, False, s < 8)

    slots_x = {}

    def b_spans(batch):
        lo, hi = batch[0], batch[-1]
        n = hi - lo + 1
        if lo == 0 or lo == 8:
            return [(pl.ds(lo, 1), batch)]
        return [(pl.ds(16 - hi, n), batch), (pl.ds(lo, n), batch)]

    def x_send(batch):
        cols = b_cols(batch[0])
        for k, (o, _) in enumerate(b_spans(batch)):
            base = slots_x[batch, k] = recv_slots(3)
            blk = wbuf.at[o, x, :, cols]
            copy(blk, blk, base + 0, at_x(1))
            copy(blk, blk, base + 1, at_x(3))

    def x_pass(batch):
        cols = b_cols(batch[0])
        for k, (o, _) in enumerate(b_spans(batch)):
            base = slots_x[batch, k]
            arrived(wbuf.at[o, left, :, cols], base + 0)
            blk = wbuf.at[o, left, rows1, cols]
            copy(blk, blk, base + 2, at_x(1))
            arrived(wbuf.at[o, right, :, cols], base + 1)
            blk = wbuf.at[o, right, rows2, cols]
            copy(blk, blk, base + 2, at_x(3))

    def x_end(batch):
        cols = b_cols(batch[0])
        for k, (o, _) in enumerate(b_spans(batch)):
            base = slots_x[batch, k]
            arrived(wbuf.at[o, far, :, cols], base + 2)

    half = (pl.ds(0, 256), pl.ds(256, 256))
    iR, iL, iF, iS = recv_slots(2), recv_slots(2), recv_slots(2), recv_slots(7)

    def ihead(d):
        return ((y + d) % NY) * 2 + c

    i_own = pltpu.make_async_copy(inp_ref, inpb.at[head], load_sem.at[5])

    def input_begin():
        i_own.start()
        copy(inp_ref.at[:, half[0]], inpb.at[head, :, half[0]], iR + 0, at_y(1))
        copy(inp_ref.at[:, half[1]], inpb.at[head, :, half[1]], iL + 1, at_y(3))
        copy(inp_ref.at[:, half[1]], inpb.at[head, :, half[1]], iR + 1, at_y(1))
        copy(inp_ref.at[:, half[0]], inpb.at[head, :, half[0]], iL + 0, at_y(3))
        copy(inp_ref, inpb.at[head], iS + 0, sib)

    def input_pass(part):
        left, right, far = ihead(3), ihead(1), ihead(2)
        if part == 0:
            arrived(inpb.at[left, :, half[0]], iR + 0)
            copy(inpb.at[left, :, half[0]], inpb.at[left, :, half[0]], iF + 0, at_y(1))
            arrived(inpb.at[right, :, half[1]], iL + 1)
            copy(inpb.at[right, :, half[1]], inpb.at[right, :, half[1]], iF + 1, at_y(3))
            copy(inpb.at[left, :, half[0]], inpb.at[left, :, half[0]], iS + 1, sib)
            copy(inpb.at[right, :, half[1]], inpb.at[right, :, half[1]], iS + 2, sib)
        if part == 1:
            arrived(inpb.at[left, :, half[1]], iR + 1)
            copy(inpb.at[left, :, half[1]], inpb.at[left, :, half[1]], iS + 3, sib)
            arrived(inpb.at[right, :, half[0]], iL + 0)
            copy(inpb.at[right, :, half[0]], inpb.at[right, :, half[0]], iS + 4, sib)
        if part == 2:
            for k in (0, 1):
                arrived(inpb.at[far, :, half[k]], iF + k)
                copy(inpb.at[far, :, half[k]], inpb.at[far, :, half[k]], iS + 5 + k, sib)
        if part == 3:
            i_own.wait()

            def other(d):
                return ((y + d) % NY) * 2 + (1 - c)
            arrived(inpb.at[other(0)], iS + 0)
            arrived(inpb.at[other(3), :, half[0]], iS + 1)
            arrived(inpb.at[other(1), :, half[1]], iS + 2)
            arrived(inpb.at[other(3), :, half[1]], iS + 3)
            arrived(inpb.at[other(1), :, half[0]], iS + 4)
            for k in (0, 1):
                arrived(inpb.at[other(2), :, half[k]], iS + 5 + k)

    lane = iota((SPAN, 128), 1)
    low = lane < 64
    lowrow = iota((1, 128), 1) < 64
    ti, tj = iota((SPAN, SPAN), 0), iota((SPAN, SPAN), 1)
    upto = ti <= tj

    def pair(col, i):
        return jnp.where(low, col[:, 2 * i:2 * i + 1], col[:, 2 * i + 1:2 * i + 2])

    def pair_row(row, i):
        return jnp.where(lowrow, row[:, 2 * i:2 * i + 1], row[:, 2 * i + 1:2 * i + 2])

    def first(sp):
        rows = pl.ds(sp * SPAN, SPAN)
        rr = mm(ld_ref[:, rows], upto.astype(F32), EXACT)
        rc = jnp.concatenate([rr, jnp.zeros((120, SPAN), F32)], 0).T
        rr_ref[sp] = rr
        rc_ref[sp] = rc
        last = rc[SPAN - 1:SPAN, :]
        ec, tc, al = jnp.exp(rc), jnp.exp(last - rc), jnp.exp(last)
        ct = c_ref[rows, :].T
        for i in range(4):
            cols = pl.ds(i * 128, 128)
            v = (g_ref[rows, cols].astype(F32) * pair(ec, i)).astype(BF)
            v_ref[rows, cols] = v
            te_ref[rows, cols] = pair(tc, i)
            a_ref[sp, i] = jnp.broadcast_to(pair_row(al, i), (8, 128))
            gst[sp, i] = mm(ct, v)
        mt_ref[sp] = mm_nt(b_ref[rows, :], c_ref[rows, :])

    def unit1(sp, i):
        rows, cols = pl.ds(sp * SPAN, SPAN), pl.ds(i * 128, 128)
        g2 = g_ref[rows, cols]
        mt = mt_ref[sp]
        parts = []
        for k in (0, 1):
            h = 2 * i + k
            diff = rr_ref[sp, h:h + 1, :] - rc_ref[sp, :, h:h + 1]
            lt = jnp.exp(jnp.where(upto, diff, NEG))
            lt_ref[sp * 8 + h] = lt
            parts.append(mm((lt * mt).astype(BF), g2))
        skip = jnp.where(lowrow, sk_ref[2 * i], sk_ref[2 * i + 1])
        gxf[rows, cols] = jnp.where(low, parts[0], parts[1]) + skip * g2.astype(F32)

    def scan_x_send(which, state):
        base = recv_slots(1)
        for i in range(4):
            sx_ref[which, i] = state(i).astype(BF)
        for d in (1, 3, 2):
            to = (x + d) % NX
            copy(sx_ref.at[which, to], xr.at[which, x], base, at_x(d))
        xr[which, x] = sx_ref[which, x]
        return base

    def scan_x_wait(which, base):
        arrived(xr.at[which, pl.ds(0, NX - 1)], base)

    def scan_z_send(which):
        base = recv_slots(1)
        for d in FAR_FIRST:
            to = (z + d) % NZ
            copy(tz.at[which, to], zr.at[which, z], base, at_z(d))
        zr[which, z] = tz[which, z]
        return base

    def scan_z_wait(which, base):
        arrived(zr.at[which, pl.ds(0, NZ - 1)], base)

    def scan_z_back(which):
        base = recv_slots(1)
        for d in FAR_FIRST:
            to = (z + d) % NZ
            copy(zo.at[which, to], zp.at[which, z], base, at_z(d))
        zp[which, z] = zo[which, z]
        return base

    def scan_z_back_wait(which, base):
        arrived(zp.at[which, pl.ds(0, NZ - 1)], base)

    def scan_x_back(which):
        base = recv_slots(1)
        for d in (1, 3, 2):
            to = (x + d) % NX
            copy(bo_ref.at[which, to], br_ref.at[which, x], base, at_x(d))
        br_ref[which, x] = bo_ref[which, x]
        return base

    def scan_x_back_wait(which, base):
        arrived(br_ref.at[which, pl.ds(0, NX - 1)], base)

    marks = {}

    def ret_x():
        base = recv_slots(1)
        for i in range(4):
            adev[i] = a_ref[0, i] * a_ref[1, i]
        for d in (1, 3, 2):
            to = (x + d) % NX
            copy(adev.at[to], ax_ref.at[x], base, at_x(d))
        ax_ref[x] = adev[x]
        marks["ax"] = base

    def ret_z():
        arrived(ax_ref.at[pl.ds(0, NX - 1)], marks["ax"])
        base = recv_slots(1)
        adev[4] = ax_ref[0] * ax_ref[1] * ax_ref[2] * ax_ref[3]
        for d in FAR_FIRST:
            copy(adev.at[4], az_ref.at[z], base, at_z(d))
        az_ref[z] = adev[4]
        marks["az"] = base

    def ret_wait():
        arrived(az_ref.at[pl.ds(0, NZ - 1)], marks["az"])

    def ret(k):
        return ax_ref[k][0:1, :]

    def put_total(which, total):
        for k in range(NZ):
            tz[which, k] = total[8 * k:8 * k + 8, :]

    def bscan(part):
        if part == 0:
            marks["b0"] = scan_x_send(0, lambda i: gst[0, i] + a_ref[0, i][0:1, :] * gst[1, i])
        if part == 1:
            scan_x_wait(0, marks["b0"])
            total = xr[0, 3].astype(F32)
            for k in (2, 1, 0):
                total = xr[0, k].astype(F32) + ret(k) * total
            put_total(0, total)
            marks["b1"] = scan_z_send(0)
        if part == 2:
            ret_wait()
            scan_z_wait(0, marks["b1"])
            q = jnp.zeros((8, 128), F32)
            for k in range(NZ - 1, -1, -1):
                zo[0, k] = q
                q = zr[0, k] + az_ref[k] * q
            marks["b2"] = scan_z_back(0)
        if part == 3:
            scan_z_back_wait(0, marks["b2"])
            q = jnp.concatenate([zp[0, k] for k in range(NZ)], 0)
            for k in (3, 2, 1, 0):
                bo_ref[0, k] = q.astype(BF)
                if k:
                    q = xr[0, k].astype(F32) + ret(k) * q
            marks["b3"] = scan_x_back(0)
        if part == 4:
            scan_x_back_wait(0, marks["b3"])
            for i in range(4):
                cols = pl.ds(i * 128, 128)
                q = br_ref[0, i]
                qs[1, :, cols] = q
                qs[0, :, cols] = (gst[1, i] + a_ref[1, i][0:1, :] * q.astype(F32)).astype(BF)

    def fscan(part):
        if part == 1:
            scan_x_wait(1, marks["f0"])
            total = xr[1, 0].astype(F32)
            for k in (1, 2, 3):
                total = xr[1, k].astype(F32) + ret(k) * total
            put_total(1, total)
            marks["f1"] = scan_z_send(1)
        if part == 2:
            scan_z_wait(1, marks["f1"])
            s = jnp.zeros((8, 128), F32)
            for k in range(NZ):
                zo[1, k] = s
                s = zr[1, k] + az_ref[k] * s
            marks["f2"] = scan_z_back(1)
        if part == 3:
            scan_z_back_wait(1, marks["f2"])
            s = jnp.concatenate([zp[1, k] for k in range(NZ)], 0)
            for k in range(NX):
                bo_ref[1, k] = s.astype(BF)
                if k < NX - 1:
                    s = xr[1, k].astype(F32) + ret(k) * s
            marks["f3"] = scan_x_back(1)
        if part == 4:
            scan_x_back_wait(1, marks["f3"])
            for i in range(4):
                cols = pl.ds(i * 128, 128)
                s = br_ref[1, i]
                ss[0, :, cols] = s
                ss[1, :, cols] = (a_ref[0, i][0:1, :] * s.astype(F32) + est[0, i]).astype(BF)

    def finish_gx(sp):
        rows = pl.ds(sp * SPAN, SPAN)
        gx[rows, :] = (gxf[rows, :] + te_ref[rows, :] * mm(b_ref[rows, :], qs[sp])).astype(BF)

    def project(first_o, count):
        def one(k, carry):
            o = (first_o + k) % NZ
            zz = (z + o) % NZ
            cols = pl.ds(pl.multiple_of((zz % 2) * 256, 256), 256)
            xacc[...] += mm(inpb[zz // 2, :, cols], wbuf[o].reshape(256, 512))
            return carry

        lax.fori_loop(0, count, one, 0)

    def own_states():
        xb = xacc[...].astype(BF)
        x_ref[...] = xb
        bt = [b_ref[pl.ds(sp * SPAN, SPAN), :].T for sp in range(2)]
        marks["f0"] = recv_slots(1)
        for d in (2, 1, 3, 0):
            to = (x + d) % NX
            cols = pl.ds(pl.multiple_of(to * 128, 128), 128)
            ex_ref[:, cols] = (te_ref[:, cols] * x_ref[:, cols].astype(F32)).astype(BF)
            for sp in range(2):
                est[sp, to] = mm(bt[sp], ex_ref[pl.ds(sp * SPAN, SPAN), cols])
            sx_ref[1, to] = (a_ref[1, to][0:1, :] * est[0, to] + est[1, to]).astype(BF)
            if d:
                copy(sx_ref.at[1, to], xr.at[1, x], marks["f0"], at_x(d))
            else:
                xr[1, x] = sx_ref[1, x]

    rS = recv_slots(4)

    def part_of(j, k):
        return mm_nt(gx[...], wbuf[(2 * j + k + NZ - z) % NZ].reshape(256, 512))

    def rs_sib(d):
        j = ((y + d) % NY) * 2 + (1 - c)
        for k in (0, 1):
            pbuf[j, :, half[k]] = part_of(j, k).astype(BF)
        copy(pbuf.at[j], sibr.at[(y + d) % NY], rS + d, sib)

    rF, rN = recv_slots(2), recv_slots(4)

    def rs_own(d):
        yy = (y + d) % NY
        j = yy * 2 + c
        arrived(sibr.at[yy], rS + d)
        for k in (0, 1):
            pbuf[j, :, half[k]] = (part_of(j, k) + sibr[yy, :, half[k]].astype(F32)).astype(BF)
        if d == 2:
            copy(pbuf.at[j, :, half[1]], yfar.at[:, half[1]], rF + 1, at_y(1))
            copy(pbuf.at[j, :, half[0]], yfar.at[:, half[0]], rF + 0, at_y(3))
        if d == 1:
            copy(pbuf.at[j, :, half[0]], ynear.at[0, :, half[0]], rN + 0, at_y(1))
        if d == 3:
            copy(pbuf.at[j, :, half[1]], ynear.at[1, :, half[1]], rN + 1, at_y(3))

    def rs_pass():
        j = ((y + 1) % NY) * 2 + c
        arrived(yfar.at[:, half[1]], rF + 1)
        pbuf[j, :, 256:512] = (pbuf[j, :, 256:512].astype(F32) + yfar[:, 256:512].astype(F32)).astype(BF)
        copy(pbuf.at[j, :, half[1]], ynear.at[0, :, half[1]], rN + 2, at_y(1))
        j = ((y + 3) % NY) * 2 + c
        arrived(yfar.at[:, half[0]], rF + 0)
        pbuf[j, :, 0:256] = (pbuf[j, :, 0:256].astype(F32) + yfar[:, 0:256].astype(F32)).astype(BF)
        copy(pbuf.at[j, :, half[0]], ynear.at[1, :, half[0]], rN + 3, at_y(3))

    def rs_end():
        arrived(ynear.at[0, :, half[0]], rN + 0)
        arrived(ynear.at[1, :, half[1]], rN + 1)
        arrived(ynear.at[0, :, half[1]], rN + 2)
        arrived(ynear.at[1, :, half[0]], rN + 3)
        gi_ref[...] = (
            pbuf[head].astype(F32) + ynear[0].astype(F32) + ynear[1].astype(F32)
        ).astype(BF)

    def unit2(sp):
        rows = pl.ds(sp * SPAN, SPAN)
        dmt[sp] = jnp.zeros((SPAN, SPAN), F32)
        dcol[sp] = jnp.zeros((SPAN, 128), F32)

        def one(i, carry):
            cols = pl.ds(pl.multiple_of(i * 128, 128), 128)
            g2, x2 = g_ref[rows, cols], x_ref[rows, cols]
            mt = mt_ref[sp]
            for k in (0, 1):
                h = 2 * i + k
                xm = jnp.where(low if k == 0 else jnp.logical_not(low), x2, jnp.zeros_like(x2))
                p = mm_nt(xm, g2) * lt_ref[sp * 8 + h]
                dmt[sp] += p
                wm = p * mt
                drow[sp, pl.ds(h, 1), :] = jnp.sum(wm, axis=0, keepdims=True)
                dcol[sp] += jnp.where(lane == h, jnp.sum(wm, axis=1, keepdims=True), 0.0)
            return carry

        lax.fori_loop(0, 4, one, 0)

    ind = (iota((8, 512), 1) // 64 == iota((8, 512), 0)).astype(BF)

    def head_sums(value):
        hi = value.astype(BF)
        lo = (value - hi.astype(F32)).astype(BF)
        return mm_nt(ind, hi) + mm_nt(ind, lo)

    def grad_b_part(sp):
        rows = pl.ds(sp * SPAN, SPAN)
        pr[0, rows, :] = (mm(dmt[sp].astype(BF), c_ref[rows, :]) + mm_nt(ex_ref[rows, :], qs[sp])).astype(BF)

    def grad_c_inner(sp):
        rows = pl.ds(sp * SPAN, SPAN)
        gc_ref[rows, :] = mm_tn(dmt[sp].astype(BF), b_ref[rows, :])

    def grad_c_part(sp):
        rows = pl.ds(sp * SPAN, SPAN)
        pr[1, rows, :] = (gc_ref[rows, :] + mm_nt(v_ref[rows, :], ss[sp])).astype(BF)

    def decay_part(sp):
        rows = pl.ds(sp * SPAN, SPAN)
        u = mm(c_ref[rows, :], ss[sp])
        arow = jnp.concatenate([a_ref[sp, i][0:1, :] for i in range(4)], 1)
        cross = jnp.sum(qs[sp].astype(F32) * ss[sp].astype(F32), axis=0, keepdims=True) * arow
        is_last = iota((SPAN, 512), 0) == SPAN - 1
        vv = v_ref[rows, :].astype(F32) * u + jnp.where(is_last, cross, 0.0)
        tt = te_ref[rows, :] * x_ref[rows, :].astype(F32) * mm(b_ref[rows, :], qs[sp])
        dr = head_sums(vv) + drow[sp] - dcol[sp].T[0:8, :]
        gld_ref[:, rows] = mm(dr, (ti >= tj).astype(F32), EXACT) + mm(head_sums(tt), (ti < tj).astype(F32), EXACT)

    def mine(k):
        return pl.ds(pl.multiple_of(k * 64, 64), 64)

    def ps_send(which):
        base = recv_slots(1)
        for d in (4, 3, 5, 2, 6, 1, 7):
            to = (head + d) % 8
            copy(pr.at[which, mine(to), :], prr.at[which, head], base, at_head(d))
        prr[which, head] = pr[which, mine(head), :]
        return base

    def ps_sum(which, base):
        arrived(prr.at[which, pl.ds(0, 7)], base)
        total = prr[which, 0].astype(F32)
        for k in range(1, 8):
            total = total + prr[which, k].astype(F32)
        pfin[which] = total.astype(BF)
        base = recv_slots(1)
        for d in (4, 3, 5, 2, 6, 1, 7):
            copy(pfin.at[which], pfull.at[which, mine(head), :], base, at_head(d))
        pfull[which, mine(head), :] = pfin[which]
        return base

    def ps_end(which, base, out):
        arrived(pfull.at[which, pl.ds(0, 448), :], base)
        out[...] = pfull[which].astype(F32)

    stores = []

    def put(src, dst):
        d = pltpu.make_async_copy(src, dst, load_sem.at[6 + len(stores)])
        d.start()
        stores.append(d)

    w_begin()
    input_begin()
    for d in loads:
        d.wait()
    w_own.wait()
    x_send((0,))
    first(0)
    p_start()
    b_step(1)
    first(1)
    ret_x()
    bscan(0)
    b_step(2)
    x_send((1, 2))
    xacc[...] = jnp.zeros_like(xacc)
    p_step(1)
    unit1(0, 0)
    b_step(3)
    x_send((3,))
    x_pass((0,))
    p_step(2)
    unit1(0, 1)
    b_step(4)
    x_pass((1, 2))
    x_end((0,))
    ret_z()
    bscan(1)
    input_pass(0)
    x_pass((3,))
    p_step(3)
    unit1(0, 2)
    b_step(5)
    x_send((4, 5))
    x_end((1, 2))
    x_end((3,))
    q_start()
    p_step(4)
    unit1(0, 3)
    b_step(6)
    x_send((6,))
    x_pass((4, 5))
    q_step(4)
    bscan(2)
    input_pass(1)
    p_step(5)
    unit1(1, 0)
    b_step(7)
    x_send((7,))
    x_pass((6,))
    q_step(5)
    p_step(6)
    unit1(1, 1)
    b_step(8)
    x_send((8,))
    x_end((4, 5))
    x_pass((7,))
    q_step(6)
    bscan(3)
    input_pass(2)
    p_step(7)
    unit1(1, 2)
    x_end((6,))
    x_pass((8,))
    q_step(7)
    unit1(1, 3)
    input_pass(3)
    project(NZ - 6, 13)
    p_step(8)
    x_end((7,))
    x_end((8,))
    q_step(8)
    project(7, 3)
    own_states()
    bscan(4)
    finish_gx(0)
    finish_gx(1)
    rs_sib(2)
    rs_sib(1)
    rs_own(2)
    fscan(1)
    rs_sib(3)
    rs_own(1)
    rs_sib(0)
    rs_own(3)
    rs_own(0)
    unit2(0)
    fscan(2)
    unit2(1)
    grad_b_part(0)
    grad_b_part(1)
    pb = ps_send(0)
    grad_c_inner(0)
    grad_c_inner(1)
    rs_pass()
    fscan(3)
    pb = ps_sum(0, pb)
    fscan(4)
    grad_c_part(0)
    grad_c_part(1)
    pc = ps_send(1)
    decay_part(0)
    pc = ps_sum(1, pc)
    decay_part(1)
    put(gld_ref, gld_hbm)
    ps_end(0, pb, gb_ref)
    put(gb_ref, gb_hbm)
    rs_end()
    put(gi_ref, gi_hbm)
    ps_end(1, pc, gc_ref)
    put(gc_ref, gc_hbm)
    for d in stores:
        d.wait()
    for d in sent[-N_SEND:]:
        d.wait_send()
    assert counts["r"] == N_RECV, counts


def local(inputs, w_in, b_rows, c_rows, log_decay, skip_gain, grad_out):
    hbm = pl.BlockSpec(memory_space=pl.ANY)
    V = pltpu.VMEM
    return pl.pallas_call(
        kernel,
        out_shape=(
            jax.ShapeDtypeStruct((T, 512), BF),
            jax.ShapeDtypeStruct((T, 128), F32),
            jax.ShapeDtypeStruct((T, 128), F32),
            jax.ShapeDtypeStruct((8, T), F32),
        ),
        in_specs=[hbm] * 5 + [pl.BlockSpec(memory_space=pltpu.SMEM), hbm],
        out_specs=(hbm,) * 4,
        scratch_shapes=[
            V((T, 128), BF),
            V((T, 128), BF),
            V((8, T), F32),
            V((T, 512), BF),
            V((T, 512), BF),
            V((T, 128), F32),
            V((T, 128), F32),
            V((8, T), F32),
            V((NZ, NX, 64, 512), BF),
            V((8, T, 512), BF),
            V((8, T, 512), BF),
            V((4, T, 512), BF),
            V((T, 512), BF),
            V((2, T, 512), BF),
            V((16, SPAN, SPAN), F32),
            V((2, SPAN, SPAN), F32),
            V((T, 512), F32),
            V((T, 512), BF),
            V((T, 512), F32),
            V((T, 512), BF),
            V((T, 512), F32),
            V((T, 512), BF),
            V((T, 512), BF),
            V((2, 8, SPAN), F32),
            V((2, SPAN, 128), F32),
            V((2, 4, 8, 128), F32),
            V((5, 8, 128), F32),
            V((4, 8, 128), F32),
            V((16, 8, 128), F32),
            V((2, 4, 128, 128), F32),
            V((2, 4, 128, 128), F32),
            V((2, 128, 512), BF),
            V((2, 128, 512), BF),
            V((2, 4, 128, 128), BF),
            V((2, 4, 128, 128), BF),
            V((2, 16, 8, 128), F32),
            V((2, 16, 8, 128), F32),
            V((2, 16, 8, 128), F32),
            V((2, 16, 8, 128), F32),
            V((2, 4, 128, 128), BF),
            V((2, 4, 128, 128), BF),
            V((2, SPAN, SPAN), F32),
            V((2, 8, SPAN), F32),
            V((2, SPAN, 128), F32),
            V((2, T, 128), BF),
            V((2, 8, 64, 128), BF),
            V((2, 64, 128), BF),
            V((2, T, 128), BF),
            pltpu.SemaphoreType.DMA((N_SEND,)),
            pltpu.SemaphoreType.DMA((N_RECV,)),
            pltpu.SemaphoreType.DMA((10,)),
        ],
        compiler_params=pltpu.CompilerParams(
            collective_id=0, has_side_effects=True, vmem_limit_bytes=60 * 1024 * 1024
        ),
        cost_estimate=pl.CostEstimate(flops=8 * 10**9, bytes_accessed=4 * 10**6, transcendentals=2 * 10**6),
    )(inputs, w_in, b_rows, c_rows, log_decay, skip_gain, grad_out)


def solution(mesh):
    in_specs = (
        P("ctx", "head"),
        P("ctx", "head"),
        P("ctx", None),
        P("ctx", None),
        P("head", "ctx"),
        P("head"),
        P("ctx", "head"),
    )
    out_specs = (P("ctx", "head"), P("ctx", None), P("ctx", None), P("head", "ctx"))
    return jax.shard_map(local, mesh=mesh, in_specs=in_specs, out_specs=out_specs, check_vma=False)
```
